256 devices in a mesh: energy: 64 (over z, y, core), slab: 4 (over x).
Axes of the slice: x: 4, y: 4, z: 8, core: 2. Of those that a mesh axis runs over, the one named last changes fastest.
Arguments:
- inv_diag: bfloat16 [2, 128, 16, 128, 128], P(None, 'energy', 'slab'), may hold values from -2 to 2, as said below
- coupling: bfloat16 [16, 128, 128], P('slab'), may hold values from -1 to 1
- tile_rows: int32 [16, 16], P('slab'), may hold values from 0 to 127, as said below
- tile_count: int32 [16], P('slab'), may hold values from 1 to 16, 160 in all
- kernel: bfloat16 [2, 255], replicated, may hold values from -0.5 to 0.5
Outputs:
- g_diag: float32 [2, 128, 16, 128, 128], P(None, 'energy', 'slab')
- self_energy: bfloat16 [2, 128, 16, 16, 128], P(None, 'energy', 'slab')
The draws below stay inside these ranges and needn't reach their ends.
Inputs may be any that keep to these rules, and one draw needn't show every extreme that they name: `inv_diag`: complex blocks with a diagonal part and full off-diagonal entries. `tile_rows`: within one slab the 16 entries are distinct. `tile_count`: the counts add up to 160.
All inputs are finite; a program needn't handle non-finite values. No bound on the sum of `tile_count` on one device may be relied on, other than what follows from the above.
Results may differ from the reference program's by a relative error of at most 0.0057.
Values may be sent and summed in bfloat16 or wider, within the bound.
A program may use at most 64 MiB of HBM per device.

```python
import math
import jax
import jax.numpy as jnp
import numpy as np
from jax import lax

ORB = 128
NT = 16
NE = 128
NSLAB = 16


def draw_inv_diag(key, part):
    key = jax.random.fold_in(key, 11)
    key_off, key_real, key_imag = jax.random.split(key, 3)
    array_shape = (2, NE, NSLAB, ORB, ORB)
    off_diagonal = jax.random.normal(key_off, array_shape, jnp.float32) * (0.4 / math.sqrt(ORB))
    real_diag = jnp.exp(jax.random.uniform(key_real, (NE, NSLAB, ORB), jnp.float32, math.log(0.75), math.log(1.05)))
    imag_diag = jax.random.uniform(key_imag, (NE, NSLAB, ORB), jnp.float32, -0.35, 0.35)
    identity = jnp.eye(ORB, dtype=jnp.float32)
    diagonal_part = jnp.stack((real_diag, imag_diag))[..., None] * identity
    return (off_diagonal + diagonal_part).astype(jnp.bfloat16)


def draw_coupling(key, part):
    key = jax.random.fold_in(key, 31)
    key_rate, key_slab, key_sign, key_noise = jax.random.split(key, 4)
    rates = jnp.exp(jax.random.uniform(key_rate, (1, ORB), jnp.float32, math.log(0.45), math.log(0.9)))
    noise = jnp.clip(jax.random.normal(key_noise, (NSLAB, ORB, ORB), jnp.float32), -4.0, 4.0)
    slab_factor = jax.random.uniform(key_slab, (NSLAB, ORB), jnp.float32, 0.92, 1.0)
    signs = jnp.where(jax.random.bernoulli(key_sign, 0.5, (NSLAB, ORB)), 1.0, -1.0).astype(jnp.float32)
    diagonal = rates * slab_factor * signs
    identity = jnp.eye(ORB, dtype=jnp.float32)
    return (noise * (0.25 / math.sqrt(ORB)) + diagonal[..., None] * identity).astype(jnp.bfloat16)


def draw_tile_rows(key, part):
    key = jax.random.fold_in(key, 23)
    slab_keys = jax.random.split(key, NSLAB)

    def one_slab(slab_key):
        return jax.random.permutation(slab_key, ORB)[:NT].astype(jnp.int32)
    chosen = jax.vmap(one_slab)(slab_keys)
    middle_rows = (jax.random.permutation(jax.random.fold_in(key, 5), ORB - 2)[:NT - 2] + 1).astype(jnp.int32)
    ends = jnp.array([0, ORB - 1], dtype=jnp.int32)
    first_slab = jax.random.permutation(jax.random.fold_in(key, 7), jnp.concatenate([ends, middle_rows])).astype(jnp.int32)
    return chosen.at[0].set(first_slab)


def profile(number_of, total, bound, lean):
    weights = [(1 << 20) // math.isqrt(rank ** lean) + 1 for rank in range(2, number_of + 1)]
    surplus, given = total - bound - (number_of - 1), [1] * (number_of - 1)
    while surplus > 0:
        free = [i for i in range(number_of - 1) if given[i] < bound]
        pool, remaining = sum([weights[i] for i in free]), surplus
        for i in free:
            more = min(bound - given[i], max(1, remaining * weights[i] // pool), surplus)
            given[i] = given[i] + more
            surplus = surplus - more
    return np.array([bound] + given)


def uneven_parts(rng, amount, total, limit, lean):
    if amount == 2:
        one = jax.random.randint(rng, (), max(1, total - limit), min(limit, total - 1) + 1)
        return jnp.stack([one, total - one])
    tallies = jnp.asarray(profile(amount, total, limit, lean), jnp.int32)
    twos = (amount - 1) // 2
    donor, sink = tallies[1:1 + 2 * twos:2], tallies[2:2 + 2 * twos:2]
    slack = jnp.minimum(donor - 1, limit - sink)
    passed = jax.random.randint(jax.random.fold_in(rng, 1), (twos,), 0, 1 << 20) % (slack + 1)
    tallies = tallies.at[1:1 + 2 * twos:2].set(donor - passed).at[2:2 + 2 * twos:2].set(sink + passed)
    return tallies[jax.random.permutation(jax.random.fold_in(rng, 2), amount)]


def scatter_about(rng, extent, width, bound, kind=jnp.bfloat16):
    drawn = jax.random.normal(rng, extent, jnp.float32) * width
    return jnp.minimum(jnp.maximum(drawn, -bound), bound).astype(kind)


def setup_inputs(seed: int = 0) -> dict:
    arg_keys = jax.random.split(jax.random.key(seed), 6)
    return {
        "inv_diag": draw_inv_diag(jax.random.fold_in(arg_keys[5], 71), 0),
        "coupling": draw_coupling(jax.random.fold_in(arg_keys[5], 71), 0),
        "tile_rows": draw_tile_rows(jax.random.fold_in(arg_keys[5], 71), 0),
        "tile_count": uneven_parts(arg_keys[3], NSLAB, NSLAB * NT * 5 // 8, NT, 2).astype(jnp.int32),
        "kernel": scatter_about(arg_keys[4], (2, 2 * NE - 1), NE ** -0.5, 0.5),
    }


def complex_product(left_real, left_imag, right_real, right_imag):
    highest = lax.Precision.HIGHEST
    out_real = jnp.einsum('eij,ejk->eik', left_real, right_real, precision=highest) - jnp.einsum('eij,ejk->eik', left_imag, right_imag, precision=highest)
    out_imag = jnp.einsum('eij,ejk->eik', left_real, right_imag, precision=highest) + jnp.einsum('eij,ejk->eik', left_imag, right_real, precision=highest)
    return out_real, out_imag


def product_transposed(left_real, left_imag, right_real, right_imag):
    highest = lax.Precision.HIGHEST
    out_real = jnp.einsum('eij,ekj->eik', left_real, right_real, precision=highest) - jnp.einsum('eij,ekj->eik', left_imag, right_imag, precision=highest)
    out_imag = jnp.einsum('eij,ekj->eik', left_real, right_imag, precision=highest) + jnp.einsum('eij,ekj->eik', left_imag, right_real, precision=highest)
    return out_real, out_imag


def reference(inv_diag, coupling, tile_rows, tile_count, kernel):
    highest = lax.Precision.HIGHEST

    def advance(state, position):
        green_real, green_imag = state
        diagonal_block = lax.dynamic_index_in_dim(inv_diag, position, axis=2, keepdims=False).astype(jnp.float32)
        couple_block = lax.dynamic_index_in_dim(coupling, position, axis=0, keepdims=False).astype(jnp.float32)
        left_real = jnp.einsum('eij,jk->eik', diagonal_block[0], couple_block, precision=highest)
        left_imag = jnp.einsum('eij,jk->eik', diagonal_block[1], couple_block, precision=highest)
        middle_real, middle_imag = complex_product(left_real, left_imag, green_real, green_imag)
        outer_real, outer_imag = product_transposed(middle_real, middle_imag, left_real, left_imag)
        new_real = diagonal_block[0] + outer_real
        new_imag = diagonal_block[1] + outer_imag
        return (new_real, new_imag), (new_real, new_imag)

    zero_block = jnp.zeros((NE, ORB, ORB), jnp.float32)
    _, (all_real, all_imag) = lax.scan(advance, (zero_block, zero_block), jnp.arange(NSLAB).astype(jnp.int32))
    g_diag = jnp.stack((all_real, all_imag)).transpose(0, 2, 1, 3, 4)

    def pick_rows(green_block, selected):
        return green_block[:, selected, :]

    picked_real = jax.vmap(pick_rows)(all_real, tile_rows)
    picked_imag = jax.vmap(pick_rows)(all_imag, tile_rows)
    occupied = jnp.arange(NT)[None, :] < tile_count[:, None]
    picked = jnp.stack((picked_real, picked_imag))
    picked = jnp.where(occupied[None, :, None, :, None], picked, 0.0)
    green_tiles = picked.transpose(0, 2, 1, 3, 4).astype(jnp.bfloat16)
    flattened = green_tiles.reshape(2, NE, NSLAB * NT * ORB)
    positions = jnp.arange(NE)
    offsets = positions[:, None] - positions[None, :] + NE - 1
    matrix = kernel[:, offsets].astype(jnp.float32)
    columns = flattened.astype(jnp.float32)
    conv_real = jnp.dot(matrix[0], columns[0], preferred_element_type=jnp.float32) - jnp.dot(matrix[1], columns[1], preferred_element_type=jnp.float32)
    conv_imag = jnp.dot(matrix[0], columns[1], preferred_element_type=jnp.float32) + jnp.dot(matrix[1], columns[0], preferred_element_type=jnp.float32)
    self_energy = jnp.stack((conv_real, conv_imag)).astype(jnp.bfloat16).reshape(2, NE, NSLAB, NT, ORB)
    return g_diag, self_energy
```

```python
import functools

import jax
import jax.numpy as jnp
from jax import lax
from jax.experimental import pallas as pl
from jax.experimental.pallas import tpu as pltpu
from jax.sharding import PartitionSpec as P

MESH = pl.DeviceIdType.MESH
F32 = jnp.float32
BF16 = jnp.bfloat16


def mm(a, b):
    return lax.dot_general(a, b, (((1,), (0,)), ((), ())), preferred_element_type=F32)


def mm_t(a, b):
    return lax.dot_general(a, b, (((1,), (1,)), ((), ())), preferred_element_type=F32)


def halves(x):
    n = x.shape[1] // 2
    return x[:, :n], x[:, n:]


def block(x):
    r, i = halves(x)
    return jnp.concatenate([x, jnp.concatenate([-i, r], 1)], 0)


def block_t(x):
    r, i = halves(x)
    return jnp.concatenate(
        [jnp.concatenate([r, -i], 1), jnp.concatenate([i, r], 1)], 0
    )


def peer_order():
    offsets = [
        (min(dz, 8 - dz) + min(dy, 4 - dy), dc, dz, dy)
        for dz in range(8)
        for dy in range(4)
        for dc in range(2)
        if dz or dy or dc
    ]
    return sorted(offsets, reverse=True)


def kernel(
    d_hbm,
    coupling_hbm,
    rows_ref,
    count_ref,
    conv_ref,
    g_hbm,
    self_ref,
    d,
    coupling,
    acc,
    walk,
    walk_t,
    end,
    into,
    relay,
    far_end,
    far_walk,
    g_out,
    conv_pad,
    conv_mat,
    pick,
    pick_walk,
    base,
    stage,
    out_1,
    in_1,
    out_2,
    in_2,
    load_sem,
    chain_send,
    chain_recv,
    g_sem,
    a2a_send,
    a2a_recv,
):
    me = lax.axis_index("energy")
    slab = lax.axis_index("slab")
    peers = lax.axis_size("energy")
    n_e, n_s, orb = d.shape[1], d.shape[2], d.shape[3]
    slots = n_s * 16
    last = n_s - 1

    loads = [
        pltpu.make_async_copy(d_hbm, d, load_sem.at[0]),
        pltpu.make_async_copy(coupling_hbm, coupling, load_sem.at[1]),
    ]
    for c in loads:
        c.start()

    barrier = pltpu.get_barrier_semaphore()

    def greet(k, carry):
        pl.semaphore_signal(
            barrier,
            inc=1,
            device_id={"energy": lax.rem(me + k, peers)},
            device_id_type=MESH,
        )
        return carry

    for k in range(1, 4):
        pl.semaphore_signal(
            barrier,
            inc=1,
            device_id={"slab": lax.rem(slab + k, 4)},
            device_id_type=MESH,
        )
    lax.fori_loop(1, peers, greet, 0)
    for c in loads:
        c.wait()

    step = []
    for i in range(n_s):
        x = mm(d[:, :, i].reshape(2 * n_e * orb, orb), coupling[i]).astype(BF16)
        x = x.reshape(2, n_e, orb, orb)
        step.append([jnp.concatenate([x[0, e], x[1, e]], 1) for e in range(n_e)])
    now = []
    for e in range(n_e):
        first = jnp.concatenate([d[0, e, 0], d[1, e, 0]], 1)
        acc[e, 0] = first.astype(F32)
        now.append(first)
    for i in range(1, n_s):
        for e in range(n_e):
            lhs = step[i][e]
            mid = mm(lhs, block(now[e])).astype(BF16)
            new = jnp.concatenate([d[0, e, i], d[1, e, i]], 1).astype(F32) + mm_t(
                mid, block_t(lhs)
            )
            acc[e, i] = new
            now[e] = new.astype(BF16)
    for e in range(n_e):
        end[e] = now[e]

    pl.semaphore_wait(barrier, peers + 2)

    def push(src, dst, send, recv, to):
        return pltpu.make_async_remote_copy(
            src, dst, send, recv, device_id={"slab": to}, device_id_type=MESH
        )

    first_hop = [
        push(end.at[e], into.at[e], chain_send.at[e], chain_recv.at[e], 1)
        for e in range(n_e)
    ]
    far_hop = [
        push(end.at[e], far_end.at[e], chain_send.at[e], chain_recv.at[2 + e], 3)
        for e in range(n_e)
    ] + [
        push(walk.at[e, last], far_walk.at[e], chain_send.at[2 + e], chain_recv.at[4 + e], 3)
        for e in range(n_e)
    ]
    second_hop = [
        [
            push(relay.at[e], into.at[e], chain_send.at[2 * e + j], chain_recv.at[e], 2 + j)
            for j in range(2)
        ]
        for e in range(n_e)
    ]

    @pl.when(slab == 0)
    def _():
        for c in first_hop:
            c.start()

    @pl.when(slab == 2)
    def _():
        for c in far_hop[:n_e]:
            c.start()

    for e in range(n_e):
        walk[e, 0] = step[0][e]
        now[e] = step[0][e]
    for i in range(1, n_s):
        for e in range(n_e):
            now[e] = mm(step[i][e], block(now[e])).astype(BF16)
            walk[e, i] = now[e]

    @pl.when(slab == 2)
    def _():
        for c in far_hop[n_e:]:
            c.start()

    row_at = lax.broadcasted_iota(jnp.int32, (16, orb), 0)
    lane_at = lax.broadcasted_iota(jnp.int32, (16, orb), 1)
    for i in range(n_s):
        wanted = jnp.full((16, orb), -1, jnp.int32)
        for t in range(16):
            row = jnp.where(t < count_ref[i], rows_ref[i, t], -1)
            wanted = jnp.where(row_at == t, row, wanted)
        pick[i] = jnp.where(lane_at == wanted, 1.0, 0.0).astype(BF16)

    conv_pad[...] = jnp.zeros_like(conv_pad)
    conv_pad[0:2, 0 : 2 * orb - 1] = conv_ref[...].astype(F32)
    bands = []
    for c in range(2):
        wide = jnp.broadcast_to(conv_pad[c : c + 1, :], (orb, 2 * orb))
        bands.append(pltpu.roll(wide, orb + 1, 1, stride=1, stride_axis=0)[:, :orb])
    flipped = jnp.concatenate(
        [
            jnp.concatenate([bands[0], bands[1]], 1),
            jnp.concatenate([-bands[1], bands[0]], 1),
        ],
        0,
    ).astype(BF16)
    big = (2 * orb, 2 * orb)
    row_at = lax.broadcasted_iota(jnp.int32, big, 0)
    lane_at = lax.broadcasted_iota(jnp.int32, big, 1)
    order = jnp.where(
        lane_at == lax.rem(row_at, 2) * orb + lax.div(row_at, 2), 1.0, 0.0
    ).astype(BF16)
    conv_mat[...] = mm_t(order, mm(order, flipped).astype(BF16)).astype(BF16)

    @pl.when(slab == 0)
    def _():
        into[...] = jnp.zeros_like(into)

    @pl.when(slab == 1)
    def _():
        for e in range(n_e):
            first_hop[e].wait_recv()
            lhs = walk[e, last]
            mid = mm(lhs, block(into[e])).astype(BF16)
            relay[e] = (acc[e, last] + mm_t(mid, block_t(lhs))).astype(BF16)
            for c in second_hop[e]:
                c.start()

    @pl.when(slab == 3)
    def _():
        for c in far_hop:
            c.wait_recv()
        for e in range(n_e):
            lhs = walk[e].reshape(n_s * orb, 2 * orb)
            mid = mm(lhs, block(far_end[e])).astype(BF16).reshape(n_s, orb, 2 * orb)
            for i in range(n_s):
                acc[e, i] = acc[e, i] + mm_t(mid[i], block_t(walk[e, i]))
            walk[e] = mm(lhs, block(far_walk[e])).astype(BF16).reshape(n_s, orb, 2 * orb)

    for e in range(n_e):
        for i in range(n_s):
            walk_t[e, i] = block_t(walk[e, i])
            pick_walk[e, 16 * i : 16 * i + 16] = mm(pick[i], walk[e, i]).astype(BF16)
            whole = acc[e, i]
            high = whole.astype(BF16)
            low = (whole - high.astype(F32)).astype(BF16)
            base[e, 16 * i : 16 * i + 16] = mm(pick[i], high) + mm(pick[i], low)

    @pl.when(slab >= 2)
    def _():
        for e in range(n_e):
            second_hop[e][0].wait_recv()

    for e in range(n_e):
        mid = mm(pick_walk[e], block(into[e])).astype(BF16)
        for i in range(n_s):
            at = slice(16 * i, 16 * i + 16)
            tile = base[e, at] + mm_t(mid[at], walk_t[e, i])
            for c, part in enumerate(halves(tile)):
                stage[pl.ds(64 * i + 2 * e + c, 16, stride=4), :] = part

    z, y, core = lax.div(me, 8), lax.rem(lax.div(me, 2), 4), lax.rem(me, 2)

    def others():
        for _, dc, dz, dy in peer_order():
            there = lax.rem(core + dc, 2)
            yield lax.rem(z + dz, 8) * 8 + lax.rem(y + dy, 4) * 2 + there

    def exchange(src, dst, at):
        for j in others():
            pltpu.make_async_remote_copy(
                src.at[j],
                dst.at[me],
                a2a_send.at[at],
                a2a_recv.at[at],
                device_id={"energy": j},
                device_id_type=MESH,
            ).start()
        dst[me] = src[me]

    def all_of(ref, sem):
        most = ref.at[pl.ds(0, peers - 1)]
        return pltpu.make_async_copy(most, most, sem)

    def pack(dst):
        for j in range(slots):
            dst[j] = stage[4 * j : 4 * j + 4, :].astype(BF16)

    def unpack(src):
        for j in range(slots):
            stage[4 * j : 4 * j + 4, :] = src[j].astype(F32)

    pack(out_1)
    exchange(out_1, in_1, 0)

    writes = []
    for e in range(n_e):
        lhs = walk[e].reshape(n_s * orb, 2 * orb)
        mid = mm(lhs, block(into[e])).astype(BF16).reshape(n_s, orb, 2 * orb)
        for i in range(n_s):
            whole = acc[e, i] + mm_t(mid[i], walk_t[e, i])
            for c, part in enumerate(halves(whole)):
                g_out[c, e, i] = part
        for c in range(2):
            w = pltpu.make_async_copy(g_out.at[c, e], g_hbm.at[c, e], g_sem.at[c, e])
            w.start()
            writes.append(w)

    all_of(in_1, a2a_recv.at[0]).wait()
    unpack(in_1)
    stage[...] = mm(conv_mat[...], stage[...].astype(BF16))
    pack(out_2)
    exchange(out_2, in_2, 1)

    for w in writes:
        w.wait()

    @pl.when(slab == 0)
    def _():
        for c in first_hop:
            c.wait_send()

    @pl.when(slab == 1)
    def _():
        for pair in second_hop:
            for c in pair:
                c.wait_send()

    @pl.when(slab == 2)
    def _():
        for c in far_hop:
            c.wait_send()

    all_of(out_1, a2a_send.at[0]).wait()
    all_of(in_2, a2a_recv.at[1]).wait()
    unpack(in_2)
    for e in range(n_e):
        for c in range(2):
            part = stage[pl.ds(2 * e + c, slots, stride=4), :]
            self_ref[c, e] = part.astype(BF16).reshape(n_s, 16, orb)
    all_of(out_2, a2a_send.at[1]).wait()


def on_device(inv_diag, coupling, tile_rows, tile_count, conv):
    _, n_e, n_s, orb, _ = inv_diag.shape
    slots = n_s * 16
    anywhere = pl.BlockSpec(memory_space=pl.ANY)
    vmem = pl.BlockSpec(memory_space=pltpu.VMEM)
    smem = pl.BlockSpec(memory_space=pltpu.SMEM)
    dma = pltpu.SemaphoreType.DMA
    return pl.pallas_call(
        kernel,
        out_shape=(
            jax.ShapeDtypeStruct((2, n_e, n_s, orb, orb), F32),
            jax.ShapeDtypeStruct((2, n_e, n_s, 16, orb), BF16),
        ),
        in_specs=[anywhere, anywhere, smem, smem, vmem],
        out_specs=(anywhere, vmem),
        scratch_shapes=[
            pltpu.VMEM(inv_diag.shape, BF16),
            pltpu.VMEM(coupling.shape, BF16),
            pltpu.VMEM((n_e, n_s, orb, 2 * orb), F32),
            pltpu.VMEM((n_e, n_s, orb, 2 * orb), BF16),
            pltpu.VMEM((n_e, n_s, 2 * orb, 2 * orb), BF16),
            pltpu.VMEM((n_e, orb, 2 * orb), BF16),
            pltpu.VMEM((n_e, orb, 2 * orb), BF16),
            pltpu.VMEM((n_e, orb, 2 * orb), BF16),
            pltpu.VMEM((n_e, orb, 2 * orb), BF16),
            pltpu.VMEM((n_e, orb, 2 * orb), BF16),
            pltpu.VMEM(inv_diag.shape, F32),
            pltpu.VMEM((8, 2 * orb), F32),
            pltpu.VMEM((2 * orb, 2 * orb), BF16),
            pltpu.VMEM((n_s, 16, orb), BF16),
            pltpu.VMEM((n_e, slots, 2 * orb), BF16),
            pltpu.VMEM((n_e, slots, 2 * orb), F32),
            pltpu.VMEM((4 * slots, orb), F32),
            pltpu.VMEM((slots, 4, orb), BF16),
            pltpu.VMEM((slots, 4, orb), BF16),
            pltpu.VMEM((slots, 4, orb), BF16),
            pltpu.VMEM((slots, 4, orb), BF16),
            dma((2,)),
            dma((4,)),
            dma((6,)),
            dma((2, n_e)),
            dma((2,)),
            dma((2,)),
        ],
        compiler_params=pltpu.CompilerParams(
            collective_id=0, has_side_effects=True, vmem_limit_bytes=48 * 1024 * 1024
        ),
        name="dyson",
    )(inv_diag, coupling, tile_rows, tile_count, conv)


def solution(mesh):
    placed = (
        P(None, "energy", "slab", None, None),
        P("slab", None, None),
        P("slab", None),
        P("slab"),
        P(),
    )
    return jax.shard_map(
        on_device,
        mesh=mesh,
        in_specs=placed,
        out_specs=(P(None, "energy", "slab", None, None), P(None, "energy", "slab", None, None)),
        check_vma=False,
    )
```

```python
import functools

import jax
import jax.numpy as jnp
from jax import lax
from jax.experimental import pallas as pl
from jax.experimental.pallas import tpu as pltpu
from jax.sharding import PartitionSpec as P

MESH = pl.DeviceIdType.MESH
F32 = jnp.float32
BF16 = jnp.bfloat16


def mm(a, b):
    return lax.dot_general(a, b, (((1,), (0,)), ((), ())), preferred_element_type=F32)


def mm_t(a, b):
    return lax.dot_general(a, b, (((1,), (1,)), ((), ())), preferred_element_type=F32)


def halves(x):
    n = x.shape[1] // 2
    return x[:, :n], x[:, n:]


def block(x):
    r, i = halves(x)
    return jnp.concatenate([x, jnp.concatenate([-i, r], 1)], 0)


def block_t(x):
    r, i = halves(x)
    return jnp.concatenate(
        [jnp.concatenate([r, -i], 1), jnp.concatenate([i, r], 1)], 0
    )


def peer_order():
    offsets = [
        (min(dz, 8 - dz) + min(dy, 4 - dy), dc, dz, dy)
        for dz in range(8)
        for dy in range(4)
        for dc in range(2)
        if dz or dy or dc
    ]
    return sorted(offsets, reverse=True)


def kernel(
    d_hbm,
    coupling_hbm,
    rows_hbm,
    count_hbm,
    conv_hbm,
    g_out,
    in_2,
    d,
    coupling,
    rows_ref,
    count_ref,
    conv_ref,
    acc,
    walk,
    walk_t,
    end,
    into,
    relay,
    far_end,
    far_walk,
    conv_pad,
    conv_mat,
    pick,
    pick_walk,
    base,
    stage,
    out_1,
    in_1,
    out_2,
    load_sem,
    chain_send,
    chain_recv,
    a2a_send,
    a2a_recv,
):
    me = lax.axis_index("energy")
    slab = lax.axis_index("slab")
    peers = lax.axis_size("energy")
    n_e, n_s, orb = d.shape[1], d.shape[2], d.shape[3]
    slots = n_s * 16
    last = n_s - 1

    loads = [
        pltpu.make_async_copy(d_hbm, d, load_sem.at[0]),
        pltpu.make_async_copy(coupling_hbm, coupling, load_sem.at[1]),
        pltpu.make_async_copy(rows_hbm, rows_ref, load_sem.at[2]),
        pltpu.make_async_copy(count_hbm, count_ref, load_sem.at[3]),
        pltpu.make_async_copy(conv_hbm, conv_ref, load_sem.at[4]),
    ]
    for c in loads:
        c.start()

    barrier = pltpu.get_barrier_semaphore()

    z, y, core = lax.div(me, 8), lax.rem(lax.div(me, 2), 4), lax.rem(me, 2)

    def others():
        for _, dc, dz, dy in peer_order():
            there = lax.rem(core + dc, 2)
            yield lax.rem(z + dz, 8) * 8 + lax.rem(y + dy, 4) * 2 + there

    for k in range(1, 4):
        pl.semaphore_signal(
            barrier,
            inc=1,
            device_id={"slab": lax.rem(slab + k, 4)},
            device_id_type=MESH,
        )
    for j in others():
        pl.semaphore_signal(barrier, inc=1, device_id={"energy": j}, device_id_type=MESH)
    for c in loads:
        c.wait()

    step = []
    for i in range(n_s):
        x = mm(d[:, :, i].reshape(2 * n_e * orb, orb), coupling[i]).astype(BF16)
        x = x.reshape(2, n_e, orb, orb)
        step.append([jnp.concatenate([x[0, e], x[1, e]], 1) for e in range(n_e)])
    now = []
    for e in range(n_e):
        first = jnp.concatenate([d[0, e, 0], d[1, e, 0]], 1)
        acc[e, 0] = first.astype(F32)
        now.append(first)
    for i in range(1, n_s):
        for e in range(n_e):
            lhs = step[i][e]
            mid = mm(lhs, block(now[e])).astype(BF16)
            new = jnp.concatenate([d[0, e, i], d[1, e, i]], 1).astype(F32) + mm_t(
                mid, block_t(lhs)
            )
            acc[e, i] = new
            now[e] = new.astype(BF16)
    for e in range(n_e):
        end[e] = now[e]

    for e in range(n_e):
        walk[e, 0] = step[0][e]
        now[e] = step[0][e]
    for i in range(1, n_s):
        for e in range(n_e):
            now[e] = mm(step[i][e], block(now[e])).astype(BF16)
            walk[e, i] = now[e]

    row_at = lax.broadcasted_iota(jnp.int32, (16, orb), 0)
    lane_at = lax.broadcasted_iota(jnp.int32, (16, orb), 1)
    for i in range(n_s):
        wanted = jnp.full((16, orb), -1, jnp.int32)
        for t in range(16):
            row = jnp.where(t < count_ref[i], rows_ref[i, t], -1)
            wanted = jnp.where(row_at == t, row, wanted)
        pick[i] = jnp.where(lane_at == wanted, 1.0, 0.0).astype(BF16)

    conv_pad[...] = jnp.zeros_like(conv_pad)
    conv_pad[0:2, 0 : 2 * orb - 1] = conv_ref[...].astype(F32)
    bands = []
    for c in range(2):
        wide = jnp.broadcast_to(conv_pad[c : c + 1, :], (orb, 2 * orb))
        bands.append(pltpu.roll(wide, orb + 1, 1, stride=1, stride_axis=0)[:, :orb])
    flipped = jnp.concatenate(
        [
            jnp.concatenate([bands[0], bands[1]], 1),
            jnp.concatenate([-bands[1], bands[0]], 1),
        ],
        0,
    ).astype(BF16)
    big = (2 * orb, 2 * orb)
    row_at = lax.broadcasted_iota(jnp.int32, big, 0)
    lane_at = lax.broadcasted_iota(jnp.int32, big, 1)
    order = jnp.where(
        lane_at == lax.rem(row_at, 2) * orb + lax.div(row_at, 2), 1.0, 0.0
    ).astype(BF16)
    conv_mat[...] = mm_t(order, mm(order, flipped).astype(BF16)).astype(BF16)

    pl.semaphore_wait(barrier, peers + 2)

    def push(src, dst, send, recv, to):
        return pltpu.make_async_remote_copy(
            src, dst, send, recv, device_id={"slab": to}, device_id_type=MESH
        )

    first_hop = [
        push(end.at[e], into.at[e], chain_send.at[e], chain_recv.at[e], 1)
        for e in range(n_e)
    ]
    far_hop = [
        (
            push(end.at[e], far_end.at[e], chain_send.at[e], chain_recv.at[2 + e], 3),
            push(walk.at[e, last], far_walk.at[e], chain_send.at[2 + e], chain_recv.at[4 + e], 3),
        )
        for e in range(n_e)
    ]
    second_hop = [
        [
            push(relay.at[e], into.at[e], chain_send.at[2 * e + j], chain_recv.at[e], 2 + j)
            for j in range(2)
        ]
        for e in range(n_e)
    ]

    @pl.when(slab == 0)
    def _():
        for c in first_hop:
            c.start()

    @pl.when(slab == 2)
    def _():
        for pair in far_hop:
            for c in pair:
                c.start()

    @pl.when(slab == 0)
    def _():
        into[...] = jnp.zeros_like(into)

    @pl.when(slab == 1)
    def _():
        for e in range(n_e):
            first_hop[e].wait_recv()
            lhs = walk[e, last]
            mid = mm(lhs, block(into[e])).astype(BF16)
            relay[e] = (acc[e, last] + mm_t(mid, block_t(lhs))).astype(BF16)
            for c in second_hop[e]:
                c.start()

    @pl.when(slab == 3)
    def _():
        for e in range(n_e):
            for c in far_hop[e]:
                c.wait_recv()
            lhs = walk[e].reshape(n_s * orb, 2 * orb)
            mid = mm(lhs, block(far_end[e])).astype(BF16).reshape(n_s, orb, 2 * orb)
            for i in range(n_s):
                acc[e, i] = acc[e, i] + mm_t(mid[i], block_t(walk[e, i]))
            walk[e] = mm(lhs, block(far_walk[e])).astype(BF16).reshape(n_s, orb, 2 * orb)

    for e in range(n_e):
        for i in range(n_s):
            walk_t[e, i] = block_t(walk[e, i])
            pick_walk[e, 16 * i : 16 * i + 16] = mm(pick[i], walk[e, i]).astype(BF16)
            whole = acc[e, i]
            high = whole.astype(BF16)
            low = (whole - high.astype(F32)).astype(BF16)
            base[e, 16 * i : 16 * i + 16] = mm(pick[i], high) + mm(pick[i], low)

    for e in range(n_e):

        @pl.when(slab >= 2)
        def _():
            second_hop[e][0].wait_recv()

        mid = mm(pick_walk[e], block(into[e])).astype(BF16)
        for i in range(n_s):
            at = slice(16 * i, 16 * i + 16)
            tile = base[e, at] + mm_t(mid[at], walk_t[e, i])
            for c, part in enumerate(halves(tile)):
                stage[pl.ds(64 * i + 2 * e + c, 16, stride=4), :] = part

    def exchange(src, dst, at):
        for j in others():
            pltpu.make_async_remote_copy(
                src.at[j],
                dst.at[me],
                a2a_send.at[at],
                a2a_recv.at[at],
                device_id={"energy": j},
                device_id_type=MESH,
            ).start()
        dst[me] = src[me]

    def all_of(ref, sem):
        most = ref.at[pl.ds(0, peers - 1)]
        return pltpu.make_async_copy(most, most, sem)

    def pack(dst):
        for j in range(slots):
            dst[j] = stage[4 * j : 4 * j + 4, :].astype(BF16)

    def unpack(src):
        for j in range(slots):
            stage[4 * j : 4 * j + 4, :] = src[j].astype(F32)

    pack(out_1)
    exchange(out_1, in_1, 0)

    for e in range(n_e):
        lhs = walk[e].reshape(n_s * orb, 2 * orb)
        mid = mm(lhs, block(into[e])).astype(BF16).reshape(n_s, orb, 2 * orb)
        for i in range(n_s):
            whole = acc[e, i] + mm_t(mid[i], walk_t[e, i])
            for c, part in enumerate(halves(whole)):
                g_out[c, e, i] = part

    all_of(in_1, a2a_recv.at[0]).wait()
    unpack(in_1)
    stage[...] = mm(conv_mat[...], stage[...].astype(BF16))
    pack(out_2)
    exchange(out_2, in_2, 1)

    @pl.when(slab == 0)
    def _():
        for c in first_hop:
            c.wait_send()

    @pl.when(slab == 1)
    def _():
        for pair in second_hop:
            for c in pair:
                c.wait_send()

    @pl.when(slab == 2)
    def _():
        for pair in far_hop:
            for c in pair:
                c.wait_send()

    all_of(out_1, a2a_send.at[0]).wait()
    all_of(in_2, a2a_recv.at[1]).wait()
    all_of(out_2, a2a_send.at[1]).wait()


def finish(g, rows, g_hbm, self_hbm, stage, self_out, sem):
    copies = [
        pltpu.make_async_copy(g, g_hbm, sem.at[0]),
        pltpu.make_async_copy(self_out, self_hbm, sem.at[1]),
    ]
    copies[0].start()
    _, n_e, n_s, _, orb = self_out.shape
    slots = rows.shape[0]
    for j in range(slots):
        stage[4 * j : 4 * j + 4, :] = rows[j].astype(F32)
    for e in range(n_e):
        for c in range(2):
            part = stage[pl.ds(2 * e + c, slots, stride=4), :]
            self_out[c, e] = part.astype(BF16).reshape(n_s, 16, orb)
    copies[1].start()
    for c in copies:
        c.wait()


def on_device(inv_diag, coupling, tile_rows, tile_count, conv):
    _, n_e, n_s, orb, _ = inv_diag.shape
    slots = n_s * 16
    vmem = pl.BlockSpec(memory_space=pltpu.VMEM)
    dma = pltpu.SemaphoreType.DMA
    hbm = pl.BlockSpec(memory_space=pltpu.HBM)
    g_shape = jax.ShapeDtypeStruct(inv_diag.shape, F32)
    self_shape = jax.ShapeDtypeStruct((2, n_e, n_s, 16, orb), BF16)
    rows_shape = jax.ShapeDtypeStruct((slots, 4, orb), BF16)
    g, rows = pl.pallas_call(
        kernel,
        out_shape=(g_shape, rows_shape),
        in_specs=[hbm] * 5,
        out_specs=(vmem, vmem),
        scratch_shapes=[
            pltpu.VMEM(inv_diag.shape, BF16),
            pltpu.VMEM(coupling.shape, BF16),
            pltpu.SMEM(tile_rows.shape, jnp.int32),
            pltpu.SMEM(tile_count.shape, jnp.int32),
            pltpu.VMEM(conv.shape, BF16),
            pltpu.VMEM((n_e, n_s, orb, 2 * orb), F32),
            pltpu.VMEM((n_e, n_s, orb, 2 * orb), BF16),
            pltpu.VMEM((n_e, n_s, 2 * orb, 2 * orb), BF16),
            pltpu.VMEM((n_e, orb, 2 * orb), BF16),
            pltpu.VMEM((n_e, orb, 2 * orb), BF16),
            pltpu.VMEM((n_e, orb, 2 * orb), BF16),
            pltpu.VMEM((n_e, orb, 2 * orb), BF16),
            pltpu.VMEM((n_e, orb, 2 * orb), BF16),
            pltpu.VMEM((8, 2 * orb), F32),
            pltpu.VMEM((2 * orb, 2 * orb), BF16),
            pltpu.VMEM((n_s, 16, orb), BF16),
            pltpu.VMEM((n_e, slots, 2 * orb), BF16),
            pltpu.VMEM((n_e, slots, 2 * orb), F32),
            pltpu.VMEM((4 * slots, orb), F32),
            pltpu.VMEM((slots, 4, orb), BF16),
            pltpu.VMEM((slots, 4, orb), BF16),
            pltpu.VMEM((slots, 4, orb), BF16),
            dma((5,)),
            dma((4,)),
            dma((6,)),
            dma((2,)),
            dma((2,)),
        ],
        compiler_params=pltpu.CompilerParams(
            collective_id=0, has_side_effects=True, vmem_limit_bytes=20 * 1024 * 1024
        ),
        name="dyson",
    )(
        *[
            pltpu.with_memory_space_constraint(x, pltpu.HBM)
            for x in (inv_diag, coupling, tile_rows, tile_count, conv)
        ]
    )
    return pl.pallas_call(
        finish,
        out_shape=(g_shape, self_shape),
        in_specs=[vmem, vmem],
        out_specs=(hbm, hbm),
        scratch_shapes=[
            pltpu.VMEM((4 * slots, orb), F32),
            pltpu.VMEM(self_shape.shape, BF16),
            dma((2,)),
        ],
        compiler_params=pltpu.CompilerParams(vmem_limit_bytes=8 * 1024 * 1024),
        name="finish",
    )(g, rows)


def solution(mesh):
    placed = (
        P(None, "energy", "slab", None, None),
        P("slab", None, None),
        P("slab", None),
        P("slab"),
        P(),
    )
    return jax.shard_map(
        on_device,
        mesh=mesh,
        in_specs=placed,
        out_specs=(P(None, "energy", "slab", None, None), P(None, "energy", "slab", None, None)),
        check_vma=False,
    )
```

```python
import functools

import jax
import jax.numpy as jnp
from jax import lax
from jax.experimental import pallas as pl
from jax.experimental.pallas import tpu as pltpu
from jax.sharding import PartitionSpec as P

MESH = pl.DeviceIdType.MESH
F32 = jnp.float32
BF16 = jnp.bfloat16


def mm(a, b):
    return lax.dot_general(a, b, (((1,), (0,)), ((), ())), preferred_element_type=F32)


def mm_t(a, b):
    return lax.dot_general(a, b, (((1,), (1,)), ((), ())), preferred_element_type=F32)


def halves(x):
    n = x.shape[1] // 2
    return x[:, :n], x[:, n:]


def block(x):
    r, i = halves(x)
    return jnp.concatenate([x, jnp.concatenate([-i, r], 1)], 0)


def block_t(x):
    r, i = halves(x)
    return jnp.concatenate(
        [jnp.concatenate([r, -i], 1), jnp.concatenate([i, r], 1)], 0
    )


def peer_order():
    offsets = [
        (min(dz, 8 - dz) + min(dy, 4 - dy), dc, dz, dy)
        for dz in range(8)
        for dy in range(4)
        for dc in range(2)
        if dz or dy or dc
    ]
    return sorted(offsets, reverse=True)


def kernel(
    d_hbm,
    coupling_hbm,
    rows_hbm,
    count_hbm,
    conv_hbm,
    g_out,
    in_2,
    d,
    coupling,
    rows_ref,
    count_ref,
    conv_ref,
    acc,
    walk,
    walk_t,
    end,
    into,
    relay,
    far_end,
    far_walk,
    conv_pad,
    conv_mat,
    pick,
    pick_walk,
    base,
    stage,
    out_1,
    in_1,
    out_2,
    load_sem,
    chain_send,
    chain_recv,
    a2a_send,
    a2a_recv,
    ready,
):
    me = lax.axis_index("energy")
    slab = lax.axis_index("slab")
    peers = lax.axis_size("energy")
    n_e, n_s, orb = d.shape[1], d.shape[2], d.shape[3]
    slots = n_s * 16
    last = n_s - 1

    coupling_load = pltpu.make_async_copy(coupling_hbm, coupling, load_sem.at[0])
    slab_loads = [
        pltpu.make_async_copy(d_hbm.at[:, :, i], d.at[:, :, i], load_sem.at[1 + i])
        for i in range(n_s)
    ]
    small_loads = [
        pltpu.make_async_copy(rows_hbm, rows_ref, load_sem.at[1 + n_s]),
        pltpu.make_async_copy(count_hbm, count_ref, load_sem.at[2 + n_s]),
        pltpu.make_async_copy(conv_hbm, conv_ref, load_sem.at[3 + n_s]),
    ]
    for c in [coupling_load, slab_loads[1], slab_loads[0]] + slab_loads[2:] + small_loads:
        c.start()

    barrier = pltpu.get_barrier_semaphore()

    z, y, core = lax.div(me, 8), lax.rem(lax.div(me, 2), 4), lax.rem(me, 2)

    def others():
        for _, dc, dz, dy in peer_order():
            there = lax.rem(core + dc, 2)
            yield lax.rem(z + dz, 8) * 8 + lax.rem(y + dy, 4) * 2 + there

    for k in range(1, 4):
        pl.semaphore_signal(
            barrier,
            inc=1,
            device_id={"slab": lax.rem(slab + k, 4)},
            device_id_type=MESH,
        )

    def greet(semaphore, j):
        pl.semaphore_signal(semaphore, inc=1, device_id={"energy": j}, device_id_type=MESH)

    column = [lax.rem(z + k, 8) * 8 + lax.rem(me, 8) for k in (4, 3, 5, 2, 6, 1, 7)]
    plane = [z * 8 + lax.rem(lax.rem(me, 8) + k, 8) for k in range(1, 8)]
    for j in column + plane:
        greet(barrier, j)

    def coupled(i):
        x = mm(d[:, :, i].reshape(2 * n_e * orb, orb), coupling[i]).astype(BF16)
        x = x.reshape(2, n_e, orb, orb)
        return [jnp.concatenate([x[0, e], x[1, e]], 1) for e in range(n_e)]

    coupling_load.wait()
    slab_loads[1].wait()
    step = [None, coupled(1)]
    slab_loads[0].wait()
    now = []
    for e in range(n_e):
        first = jnp.concatenate([d[0, e, 0], d[1, e, 0]], 1)
        acc[e, 0] = first.astype(F32)
        now.append(first)
    for i in range(1, n_s):
        if i > 1:
            slab_loads[i].wait()
            step.append(coupled(i))
        for e in range(n_e):
            lhs = step[i][e]
            mid = mm(lhs, block(now[e])).astype(BF16)
            new = jnp.concatenate([d[0, e, i], d[1, e, i]], 1).astype(F32) + mm_t(
                mid, block_t(lhs)
            )
            acc[e, i] = new
            now[e] = new.astype(BF16)
            if i == last:
                end[e] = now[e]

    pl.semaphore_wait(barrier, 3 + len(column) + len(plane))
    for j in plane:
        greet(ready, j)

    def push(src, dst, send, recv, to):
        return pltpu.make_async_remote_copy(
            src, dst, send, recv, device_id={"slab": to}, device_id_type=MESH
        )

    first_hop = [
        push(end.at[e], into.at[e], chain_send.at[e], chain_recv.at[e], 1)
        for e in range(n_e)
    ]
    far_hop = [
        (
            push(end.at[e], far_end.at[e], chain_send.at[e], chain_recv.at[2 + e], 3),
            push(walk.at[e, last], far_walk.at[e], chain_send.at[2 + e], chain_recv.at[4 + e], 3),
        )
        for e in range(n_e)
    ]
    second_hop = [
        [
            push(relay.at[e], into.at[e], chain_send.at[2 * e + j], chain_recv.at[e], 2 + j)
            for j in range(2)
        ]
        for e in range(n_e)
    ]

    @pl.when(slab == 0)
    def _():
        for c in first_hop:
            c.start()

    @pl.when(slab == 2)
    def _():
        for pair in far_hop:
            pair[0].start()

    step[0] = coupled(0)
    for e in range(n_e):
        walk[e, 0] = step[0][e]
        now[e] = step[0][e]
    for i in range(1, n_s):
        for e in range(n_e):
            now[e] = mm(step[i][e], block(now[e])).astype(BF16)
            walk[e, i] = now[e]

    @pl.when(slab == 2)
    def _():
        for pair in far_hop:
            pair[1].start()

    for c in small_loads:
        c.wait()

    row_at = lax.broadcasted_iota(jnp.int32, (16, orb), 0)
    lane_at = lax.broadcasted_iota(jnp.int32, (16, orb), 1)
    for i in range(n_s):
        wanted = jnp.full((16, orb), -1, jnp.int32)
        for t in range(16):
            row = jnp.where(t < count_ref[i], rows_ref[i, t], -1)
            wanted = jnp.where(row_at == t, row, wanted)
        pick[i] = jnp.where(lane_at == wanted, 1.0, 0.0).astype(BF16)

    conv_pad[...] = jnp.zeros_like(conv_pad)
    conv_pad[0:2, 0 : 2 * orb - 1] = conv_ref[...].astype(F32)
    bands = []
    for c in range(2):
        wide = jnp.broadcast_to(conv_pad[c : c + 1, :], (orb, 2 * orb))
        bands.append(pltpu.roll(wide, orb + 1, 1, stride=1, stride_axis=0)[:, :orb])
    flipped = jnp.concatenate(
        [
            jnp.concatenate([bands[0], bands[1]], 1),
            jnp.concatenate([-bands[1], bands[0]], 1),
        ],
        0,
    ).astype(BF16)
    big = (2 * orb, 2 * orb)
    row_at = lax.broadcasted_iota(jnp.int32, big, 0)
    lane_at = lax.broadcasted_iota(jnp.int32, big, 1)
    order = jnp.where(
        lane_at == lax.rem(row_at, 2) * orb + lax.div(row_at, 2), 1.0, 0.0
    ).astype(BF16)
    conv_mat[...] = mm_t(order, mm(order, flipped).astype(BF16)).astype(BF16)

    def prepare():
        for e in range(n_e):
            for i in range(n_s):
                walk_t[e, i] = block_t(walk[e, i])
                pick_walk[e, 16 * i : 16 * i + 16] = mm(pick[i], walk[e, i]).astype(BF16)
                whole = acc[e, i]
                high = whole.astype(BF16)
                low = (whole - high.astype(F32)).astype(BF16)
                base[e, 16 * i : 16 * i + 16] = mm(pick[i], high) + mm(pick[i], low)

    @pl.when(slab != 3)
    def _():
        prepare()

    @pl.when(slab == 0)
    def _():
        into[...] = jnp.zeros_like(into)

    @pl.when(slab == 1)
    def _():
        for e in range(n_e):
            first_hop[e].wait_recv()
            lhs = walk[e, last]
            mid = mm(lhs, block(into[e])).astype(BF16)
            relay[e] = (acc[e, last] + mm_t(mid, block_t(lhs))).astype(BF16)
            for c in second_hop[e]:
                c.start()

    @pl.when(slab == 3)
    def _():
        for e in range(n_e):
            for c in far_hop[e]:
                c.wait_recv()
            lhs = walk[e].reshape(n_s * orb, 2 * orb)
            mid = mm(lhs, block(far_end[e])).astype(BF16).reshape(n_s, orb, 2 * orb)
            for i in range(n_s):
                acc[e, i] = acc[e, i] + mm_t(mid[i], block_t(walk[e, i]))
            walk[e] = mm(lhs, block(far_walk[e])).astype(BF16).reshape(n_s, orb, 2 * orb)
        prepare()

    for e in range(n_e):

        @pl.when(slab >= 2)
        def _():
            second_hop[e][0].wait_recv()

        mid = mm(pick_walk[e], block(into[e])).astype(BF16)
        for i in range(n_s):
            at = slice(16 * i, 16 * i + 16)
            tile = base[e, at] + mm_t(mid[at], walk_t[e, i])
            for c, part in enumerate(halves(tile)):
                stage[pl.ds(64 * i + 2 * e + c, 16, stride=4), :] = part

    def exchange(src, dst, at):
        for j in others():
            pltpu.make_async_remote_copy(
                src.at[j],
                dst.at[me],
                a2a_send.at[at],
                a2a_recv.at[at],
                device_id={"energy": j},
                device_id_type=MESH,
            ).start()
        dst[me] = src[me]

    def all_of(ref, sem):
        most = ref.at[pl.ds(0, peers - 1)]
        return pltpu.make_async_copy(most, most, sem)

    def pack(dst):
        for j in range(slots):
            dst[j] = stage[4 * j : 4 * j + 4, :].astype(BF16)

    def unpack(src):
        for j in range(slots):
            stage[4 * j : 4 * j + 4, :] = src[j].astype(F32)

    pack(out_1)
    pl.semaphore_wait(ready, len(plane))
    exchange(out_1, in_1, 0)

    for e in range(n_e):
        lhs = walk[e].reshape(n_s * orb, 2 * orb)
        mid = mm(lhs, block(into[e])).astype(BF16).reshape(n_s, orb, 2 * orb)
        for i in range(n_s):
            whole = acc[e, i] + mm_t(mid[i], walk_t[e, i])
            for c, part in enumerate(halves(whole)):
                g_out[c, e, i] = part

    all_of(in_1, a2a_recv.at[0]).wait()
    unpack(in_1)
    stage[...] = mm(conv_mat[...], stage[...].astype(BF16))
    pack(out_2)
    exchange(out_2, in_2, 1)

    @pl.when(slab == 0)
    def _():
        for c in first_hop:
            c.wait_send()

    @pl.when(slab == 1)
    def _():
        for pair in second_hop:
            for c in pair:
                c.wait_send()

    @pl.when(slab == 2)
    def _():
        for pair in far_hop:
            for c in pair:
                c.wait_send()

    all_of(out_1, a2a_send.at[0]).wait()
    all_of(in_2, a2a_recv.at[1]).wait()
    all_of(out_2, a2a_send.at[1]).wait()


def finish(g, rows, g_hbm, self_hbm, stage, self_out, sem):
    copies = [
        pltpu.make_async_copy(g, g_hbm, sem.at[0]),
        pltpu.make_async_copy(self_out, self_hbm, sem.at[1]),
    ]
    copies[0].start()
    _, n_e, n_s, _, orb = self_out.shape
    slots = rows.shape[0]
    for j in range(slots):
        stage[4 * j : 4 * j + 4, :] = rows[j].astype(F32)
    for e in range(n_e):
        for c in range(2):
            part = stage[pl.ds(2 * e + c, slots, stride=4), :]
            self_out[c, e] = part.astype(BF16).reshape(n_s, 16, orb)
    copies[1].start()
    for c in copies:
        c.wait()


def on_device(inv_diag, coupling, tile_rows, tile_count, conv):
    _, n_e, n_s, orb, _ = inv_diag.shape
    slots = n_s * 16
    vmem = pl.BlockSpec(memory_space=pltpu.VMEM)
    dma = pltpu.SemaphoreType.DMA
    hbm = pl.BlockSpec(memory_space=pltpu.HBM)
    g_shape = jax.ShapeDtypeStruct(inv_diag.shape, F32)
    self_shape = jax.ShapeDtypeStruct((2, n_e, n_s, 16, orb), BF16)
    rows_shape = jax.ShapeDtypeStruct((slots, 4, orb), BF16)
    g, rows = pl.pallas_call(
        kernel,
        out_shape=(g_shape, rows_shape),
        in_specs=[hbm] * 5,
        out_specs=(vmem, vmem),
        scratch_shapes=[
            pltpu.VMEM(inv_diag.shape, BF16),
            pltpu.VMEM(coupling.shape, BF16),
            pltpu.SMEM(tile_rows.shape, jnp.int32),
            pltpu.SMEM(tile_count.shape, jnp.int32),
            pltpu.VMEM(conv.shape, BF16),
            pltpu.VMEM((n_e, n_s, orb, 2 * orb), F32),
            pltpu.VMEM((n_e, n_s, orb, 2 * orb), BF16),
            pltpu.VMEM((n_e, n_s, 2 * orb, 2 * orb), BF16),
            pltpu.VMEM((n_e, orb, 2 * orb), BF16),
            pltpu.VMEM((n_e, orb, 2 * orb), BF16),
            pltpu.VMEM((n_e, orb, 2 * orb), BF16),
            pltpu.VMEM((n_e, orb, 2 * orb), BF16),
            pltpu.VMEM((n_e, orb, 2 * orb), BF16),
            pltpu.VMEM((8, 2 * orb), F32),
            pltpu.VMEM((2 * orb, 2 * orb), BF16),
            pltpu.VMEM((n_s, 16, orb), BF16),
            pltpu.VMEM((n_e, slots, 2 * orb), BF16),
            pltpu.VMEM((n_e, slots, 2 * orb), F32),
            pltpu.VMEM((4 * slots, orb), F32),
            pltpu.VMEM((slots, 4, orb), BF16),
            pltpu.VMEM((slots, 4, orb), BF16),
            pltpu.VMEM((slots, 4, orb), BF16),
            dma((n_s + 4,)),
            dma((4,)),
            dma((6,)),
            dma((2,)),
            dma((2,)),
            pltpu.SemaphoreType.REGULAR,
        ],
        compiler_params=pltpu.CompilerParams(
            collective_id=0, has_side_effects=True, vmem_limit_bytes=20 * 1024 * 1024
        ),
        name="dyson",
    )(
        *[
            pltpu.with_memory_space_constraint(x, pltpu.HBM)
            for x in (inv_diag, coupling, tile_rows, tile_count, conv)
        ]
    )
    return pl.pallas_call(
        finish,
        out_shape=(g_shape, self_shape),
        in_specs=[vmem, vmem],
        out_specs=(hbm, hbm),
        scratch_shapes=[
            pltpu.VMEM((4 * slots, orb), F32),
            pltpu.VMEM(self_shape.shape, BF16),
            dma((2,)),
        ],
        compiler_params=pltpu.CompilerParams(vmem_limit_bytes=8 * 1024 * 1024),
        name="finish",
    )(g, rows)


def solution(mesh):
    placed = (
        P(None, "energy", "slab", None, None),
        P("slab", None, None),
        P("slab", None),
        P("slab"),
        P(),
    )
    return jax.shard_map(
        on_device,
        mesh=mesh,
        in_specs=placed,
        out_specs=(P(None, "energy", "slab", None, None), P(None, "energy", "slab", None, None)),
        check_vma=False,
    )
```

```python
import functools

import jax
import jax.numpy as jnp
from jax import lax
from jax.experimental import pallas as pl
from jax.experimental.pallas import tpu as pltpu
from jax.sharding import PartitionSpec as P

MESH = pl.DeviceIdType.MESH
F32 = jnp.float32
BF16 = jnp.bfloat16


def mm(a, b):
    return lax.dot_general(a, b, (((1,), (0,)), ((), ())), preferred_element_type=F32)


def mm_t(a, b):
    return lax.dot_general(a, b, (((1,), (1,)), ((), ())), preferred_element_type=F32)


def stacked(real, imag):
    return jnp.concatenate([real, imag], 0).astype(BF16)


def beside(real, imag):
    return jnp.concatenate([real, imag], 1).astype(BF16)


def cross(x):
    h, w = x.shape[0] // 2, x.shape[1] // 2
    return x[:h, :w] - x[h:, w:], x[:h, w:] + x[h:, :w]


def times(left_stacked, right_beside):
    return cross(mm(left_stacked, right_beside))


def times_t(real, imag, right_stacked):
    return cross(mm_t(stacked(real, imag), right_stacked))


def around(outer_stacked, middle_beside):
    return times_t(*times(outer_stacked, middle_beside), outer_stacked)


def peer_order():
    offsets = [
        (min(dz, 8 - dz) + min(dy, 4 - dy), dc, dz, dy)
        for dz in range(8)
        for dy in range(4)
        for dc in range(2)
        if dz or dy or dc
    ]
    return sorted(offsets, reverse=True)


def kernel(
    d_hbm,
    coupling_hbm,
    rows_hbm,
    count_hbm,
    conv_hbm,
    g_out,
    in_2,
    d,
    coupling,
    rows_ref,
    count_ref,
    conv_ref,
    acc,
    walk,
    product,
    end,
    into,
    relay,
    far_end,
    far_walk,
    conv_pad,
    conv_mat,
    pick,
    pick_walk,
    base,
    stage,
    out_1,
    in_1,
    out_2,
    load_sem,
    chain_send,
    chain_recv,
    a2a_send,
    a2a_recv,
    lines_here,
    columns_here,
    ready,
):
    me = lax.axis_index("energy")
    slab = lax.axis_index("slab")
    peers = lax.axis_size("energy")
    n_e, n_s, orb = d.shape[1], d.shape[2], d.shape[3]
    slots = n_s * 16
    last = n_s - 1

    coupling_load = pltpu.make_async_copy(coupling_hbm, coupling, load_sem.at[0])
    slab_loads = [
        pltpu.make_async_copy(d_hbm.at[:, :, i], d.at[:, :, i], load_sem.at[1 + i])
        for i in range(n_s)
    ]
    small_loads = [
        pltpu.make_async_copy(rows_hbm, rows_ref, load_sem.at[1 + n_s]),
        pltpu.make_async_copy(count_hbm, count_ref, load_sem.at[2 + n_s]),
        pltpu.make_async_copy(conv_hbm, conv_ref, load_sem.at[3 + n_s]),
    ]
    for c in [coupling_load, slab_loads[1], slab_loads[0]] + slab_loads[2:] + small_loads:
        c.start()

    barrier = pltpu.get_barrier_semaphore()

    z, y, core = lax.div(me, 8), lax.rem(lax.div(me, 2), 4), lax.rem(me, 2)

    def others():
        for _, dc, dz, dy in peer_order():
            there = lax.rem(core + dc, 2)
            yield lax.rem(z + dz, 8) * 8 + lax.rem(y + dy, 4) * 2 + there

    for receiver, sender in ((1, 0), (2, 1), (3, 1), (3, 2), (0, 1), (2, 3)):

        @pl.when(slab == receiver)
        def _():
            pl.semaphore_signal(
                barrier, inc=1, device_id={"slab": sender}, device_id_type=MESH
            )

    odd = lax.rem(slab, 2) == 1

    def greet(semaphore, j):
        pl.semaphore_signal(semaphore, inc=1, device_id={"energy": j}, device_id_type=MESH)

    column = [lax.rem(z + k, 8) * 8 + lax.rem(me, 8) for k in (4, 3, 5, 2, 6, 1, 7)]
    plane = [z * 8 + lax.rem(lax.rem(me, 8) + k, 8) for k in range(1, 8)]

    @pl.when(odd)
    def _():
        for j in column + plane:
            greet(barrier, j)


    def coupled(i):
        x = mm(d[:, :, i].reshape(2 * n_e * orb, orb), coupling[i]).astype(BF16)
        x = x.reshape(2, n_e, orb, orb)
        return [x[:, e].reshape(2 * orb, orb) for e in range(n_e)]

    every = range(n_e)

    coupling_load.wait()
    slab_loads[1].wait()
    step = [None, coupled(1)]
    slab_loads[0].wait()
    now = [beside(d[0, e, 0], d[1, e, 0]) for e in every]

    def plus(e, i, moved):
        return [d[c, e, i].astype(F32) + moved[c] for c in range(2)]

    def keep(e, i, new):
        for c in range(2):
            acc[e, i, c] = new[c]

    second = [plus(e, 1, around(step[1][e], now[e])) for e in every]
    slab_loads[2].wait()
    step.append(coupled(2))
    slab_loads[3].wait()
    step.append(coupled(3))
    both = [
        stacked(*times(step[3][e], beside(step[2][e][:orb], step[2][e][orb:]))) for e in every
    ]
    outer = [plus(e, 3, around(step[3][e], beside(d[0, e, 2], d[1, e, 2]))) for e in every]
    for e in every:
        keep(e, 1, second[e])
        moved = around(both[e], beside(*second[e]))
        new = [outer[e][c] + moved[c] for c in range(2)]
        keep(e, 3, new)
        end[e] = beside(*new)

    around_here = len(column) + len(plane)
    first = jnp.where(odd, jnp.where(slab == 3, 1, 3) + around_here, 1)
    pl.semaphore_wait(barrier, first)

    @pl.when(odd)
    def _():
        for j in column:
            greet(lines_here, j)

    def push(src, dst, send, recv, to):
        return pltpu.make_async_remote_copy(
            src, dst, send, recv, device_id={"slab": to}, device_id_type=MESH
        )

    first_hop = [
        push(end.at[e], into.at[e], chain_send.at[e], chain_recv.at[e], 1)
        for e in range(n_e)
    ]
    far_hop = [
        (
            push(end.at[e], far_end.at[e], chain_send.at[e], chain_recv.at[2 + e], 3),
            push(product.at[e], far_walk.at[e], chain_send.at[2 + e], chain_recv.at[4 + e], 3),
        )
        for e in range(n_e)
    ]
    second_hop = [
        [
            push(relay.at[e], into.at[e], chain_send.at[2 * e + j], chain_recv.at[e], 2 + j)
            for j in range(2)
        ]
        for e in range(n_e)
    ]

    @pl.when(slab == 0)
    def _():
        for c in first_hop:
            c.start()

    @pl.when(slab == 2)
    def _():
        for pair in far_hop:
            pair[0].start()

    step[0] = coupled(0)
    for e in every:
        walk[e, 0] = step[0][e]
        now[e] = beside(step[0][e][:orb], step[0][e][orb:])
    for i in range(1, n_s):
        for e in every:
            moved = times(step[i][e], now[e])
            walk[e, i] = stacked(*moved)
            now[e] = beside(*moved)
            if i == last:
                product[e] = now[e]

    @pl.when(slab == 2)
    def _():
        for pair in far_hop:
            pair[1].start()

    for e in every:
        for c in range(2):
            acc[e, 0, c] = d[c, e, 0].astype(F32)
        keep(e, 2, plus(e, 2, around(step[2][e], beside(acc[e, 1, 0], acc[e, 1, 1]))))

    for c in small_loads:
        c.wait()

    row_at = lax.broadcasted_iota(jnp.int32, (16, orb), 0)
    lane_at = lax.broadcasted_iota(jnp.int32, (16, orb), 1)
    for i in range(n_s):
        wanted = jnp.full((16, orb), -1, jnp.int32)
        for t in range(16):
            row = jnp.where(t < count_ref[i], rows_ref[i, t], -1)
            wanted = jnp.where(row_at == t, row, wanted)
        pick[i] = jnp.where(lane_at == wanted, 1.0, 0.0).astype(BF16)

    conv_pad[...] = jnp.zeros_like(conv_pad)
    conv_pad[0:2, 0 : 2 * orb - 1] = conv_ref[...].astype(F32)
    bands = []
    for c in range(2):
        wide = jnp.broadcast_to(conv_pad[c : c + 1, :], (orb, 2 * orb))
        bands.append(pltpu.roll(wide, orb + 1, 1, stride=1, stride_axis=0)[:, :orb])
    flipped = jnp.concatenate(
        [
            jnp.concatenate([bands[0], bands[1]], 1),
            jnp.concatenate([-bands[1], bands[0]], 1),
        ],
        0,
    ).astype(BF16)
    big = (2 * orb, 2 * orb)
    row_at = lax.broadcasted_iota(jnp.int32, big, 0)
    lane_at = lax.broadcasted_iota(jnp.int32, big, 1)
    order = jnp.where(
        lane_at == lax.rem(row_at, 2) * orb + lax.div(row_at, 2), 1.0, 0.0
    ).astype(BF16)
    conv_mat[...] = mm_t(order, mm(order, flipped).astype(BF16)).astype(BF16)

    for e in every:
        for i in range(n_s):
            at = slice(16 * i, 16 * i + 16)
            own = walk[e, i]
            chosen = mm(pick[i], jnp.concatenate([own[:orb], own[orb:]], 1)).astype(BF16)
            pick_walk[e, at] = chosen[:, :orb]
            pick_walk[e, slots + 16 * i : slots + 16 * i + 16] = chosen[:, orb:]
            high = beside(acc[e, i, 0], acc[e, i, 1])
            low = beside(*[acc[e, i, c] - acc[e, i, c].astype(BF16).astype(F32) for c in range(2)])
            base[e, at] = mm(pick[i], high) + mm(pick[i], low)

    def rows_around(e, middle):
        real, imag = times(pick_walk[e], middle)
        for i in range(n_s):
            at = slice(16 * i, 16 * i + 16)
            yield i, at, times_t(real[at], imag[at], walk[e, i])

    def blocks_around(e, middle):
        mid = mm(walk[e].reshape(n_s * 2 * orb, orb), middle).reshape(n_s, 2 * orb, 2 * orb)
        for i in range(n_s):
            yield i, times_t(*cross(mid[i]), walk[e, i])

    def select(e):
        for i, at, moved in rows_around(e, into[e]):
            for c in range(2):
                part = base[e, at, c * orb : (c + 1) * orb] + moved[c]
                stage[pl.ds(64 * i + 2 * e + c, 16, stride=4), :] = part

    def lines_are_here():
        pl.semaphore_wait(lines_here, len(column))
        for j in plane:
            greet(columns_here, j)

    def all_here(to):
        pl.semaphore_wait(columns_here, len(plane))
        pl.semaphore_signal(ready, inc=1, device_id={"slab": to}, device_id_type=MESH)

    @pl.when(slab == 0)
    def _():
        into[...] = jnp.zeros_like(into)

    @pl.when(slab == 1)
    def _():
        for e in every:
            first_hop[e].wait_recv()
            moved = around(walk[e, last], into[e])
            relay[e] = beside(*[acc[e, last, c] + moved[c] for c in range(2)])
            for c in second_hop[e]:
                c.start()
            if e == 0:
                lines_are_here()
        all_here(0)

    @pl.when(slab == 3)
    def _():
        lines_are_here()
        for e in every:
            far_hop[e][0].wait_recv()
            for i, at, moved in rows_around(e, far_end[e]):
                base[e, at] = base[e, at] + jnp.concatenate(moved, 1)
            for i, moved in blocks_around(e, far_end[e]):
                for c in range(2):
                    acc[e, i, c] = acc[e, i, c] + moved[c]
        all_here(2)
        for e in every:
            far_hop[e][1].wait_recv()
            pick_walk[e] = stacked(*times(pick_walk[e], far_walk[e]))
            for i in range(n_s):
                walk[e, i] = stacked(*times(walk[e, i], far_walk[e]))

    for e in every:

        @pl.when(slab >= 2)
        def _():
            second_hop[e][0].wait_recv()

        select(e)

    def exchange(src, dst, at):
        for j in others():
            pltpu.make_async_remote_copy(
                src.at[j],
                dst.at[me],
                a2a_send.at[at],
                a2a_recv.at[at],
                device_id={"energy": j},
                device_id_type=MESH,
            ).start()
        dst[me] = src[me]

    def all_of(ref, sem):
        most = ref.at[pl.ds(0, peers - 1)]
        return pltpu.make_async_copy(most, most, sem)

    def pack(dst):
        for j in range(slots):
            dst[j] = stage[4 * j : 4 * j + 4, :].astype(BF16)

    def unpack(src):
        for j in range(slots):
            stage[4 * j : 4 * j + 4, :] = src[j].astype(F32)

    pack(out_1)

    @pl.when(jnp.logical_not(odd))
    def _():
        pl.semaphore_wait(ready, 1)

    exchange(out_1, in_1, 0)

    for e in every:
        for i, moved in blocks_around(e, into[e]):
            for c in range(2):
                g_out[c, e, i] = acc[e, i, c] + moved[c]

    all_of(in_1, a2a_recv.at[0]).wait()
    unpack(in_1)
    stage[...] = mm(conv_mat[...], stage[...].astype(BF16))
    pack(out_2)
    exchange(out_2, in_2, 1)

    @pl.when(slab == 0)
    def _():
        for c in first_hop:
            c.wait_send()

    @pl.when(slab == 1)
    def _():
        for pair in second_hop:
            for c in pair:
                c.wait_send()

    @pl.when(slab == 2)
    def _():
        for pair in far_hop:
            for c in pair:
                c.wait_send()

    all_of(out_1, a2a_send.at[0]).wait()
    all_of(in_2, a2a_recv.at[1]).wait()
    all_of(out_2, a2a_send.at[1]).wait()


def finish(g, rows, g_hbm, self_hbm, stage, self_out, sem):
    copies = [
        pltpu.make_async_copy(g, g_hbm, sem.at[0]),
        pltpu.make_async_copy(self_out, self_hbm, sem.at[1]),
    ]
    copies[0].start()
    _, n_e, n_s, _, orb = self_out.shape
    slots = rows.shape[0]
    for j in range(slots):
        stage[4 * j : 4 * j + 4, :] = rows[j].astype(F32)
    for e in range(n_e):
        for c in range(2):
            part = stage[pl.ds(2 * e + c, slots, stride=4), :]
            self_out[c, e] = part.astype(BF16).reshape(n_s, 16, orb)
    copies[1].start()
    for c in copies:
        c.wait()


def on_device(inv_diag, coupling, tile_rows, tile_count, conv):
    _, n_e, n_s, orb, _ = inv_diag.shape
    slots = n_s * 16
    vmem = pl.BlockSpec(memory_space=pltpu.VMEM)
    dma = pltpu.SemaphoreType.DMA
    hbm = pl.BlockSpec(memory_space=pltpu.HBM)
    g_shape = jax.ShapeDtypeStruct(inv_diag.shape, F32)
    self_shape = jax.ShapeDtypeStruct((2, n_e, n_s, 16, orb), BF16)
    rows_shape = jax.ShapeDtypeStruct((slots, 4, orb), BF16)
    g, rows = pl.pallas_call(
        kernel,
        out_shape=(g_shape, rows_shape),
        in_specs=[hbm] * 5,
        out_specs=(vmem, vmem),
        scratch_shapes=[
            pltpu.VMEM(inv_diag.shape, BF16),
            pltpu.VMEM(coupling.shape, BF16),
            pltpu.SMEM(tile_rows.shape, jnp.int32),
            pltpu.SMEM(tile_count.shape, jnp.int32),
            pltpu.VMEM(conv.shape, BF16),
            pltpu.VMEM((n_e, n_s, 2, orb, orb), F32),
            pltpu.VMEM((n_e, n_s, 2 * orb, orb), BF16),
            pltpu.VMEM((n_e, orb, 2 * orb), BF16),
            pltpu.VMEM((n_e, orb, 2 * orb), BF16),
            pltpu.VMEM((n_e, orb, 2 * orb), BF16),
            pltpu.VMEM((n_e, orb, 2 * orb), BF16),
            pltpu.VMEM((n_e, orb, 2 * orb), BF16),
            pltpu.VMEM((n_e, orb, 2 * orb), BF16),
            pltpu.VMEM((8, 2 * orb), F32),
            pltpu.VMEM((2 * orb, 2 * orb), BF16),
            pltpu.VMEM((n_s, 16, orb), BF16),
            pltpu.VMEM((n_e, 2 * slots, orb), BF16),
            pltpu.VMEM((n_e, slots, 2 * orb), F32),
            pltpu.VMEM((4 * slots, orb), F32),
            pltpu.VMEM((slots, 4, orb), BF16),
            pltpu.VMEM((slots, 4, orb), BF16),
            pltpu.VMEM((slots, 4, orb), BF16),
            dma((n_s + 4,)),
            dma((4,)),
            dma((6,)),
            dma((2,)),
            dma((2,)),
            pltpu.SemaphoreType.REGULAR,
            pltpu.SemaphoreType.REGULAR,
            pltpu.SemaphoreType.REGULAR,
        ],
        compiler_params=pltpu.CompilerParams(
            collective_id=0, has_side_effects=True, vmem_limit_bytes=20 * 1024 * 1024
        ),
        name="dyson",
    )(
        *[
            pltpu.with_memory_space_constraint(x, pltpu.HBM)
            for x in (inv_diag, coupling, tile_rows, tile_count, conv)
        ]
    )
    return pl.pallas_call(
        finish,
        out_shape=(g_shape, self_shape),
        in_specs=[vmem, vmem],
        out_specs=(hbm, hbm),
        scratch_shapes=[
            pltpu.VMEM((4 * slots, orb), F32),
            pltpu.VMEM(self_shape.shape, BF16),
            dma((2,)),
        ],
        compiler_params=pltpu.CompilerParams(vmem_limit_bytes=8 * 1024 * 1024),
        name="finish",
    )(g, rows)


def solution(mesh):
    placed = (
        P(None, "energy", "slab", None, None),
        P("slab", None, None),
        P("slab", None),
        P("slab"),
        P(),
    )
    return jax.shard_map(
        on_device,
        mesh=mesh,
        in_specs=placed,
        out_specs=(P(None, "energy", "slab", None, None), P(None, "energy", "slab", None, None)),
        check_vma=False,
    )
```

```python
import functools

import jax
import jax.numpy as jnp
from jax import lax
from jax.experimental import pallas as pl
from jax.experimental.pallas import tpu as pltpu
from jax.sharding import PartitionSpec as P

MESH = pl.DeviceIdType.MESH
F32 = jnp.float32
BF16 = jnp.bfloat16


def mm(a, b):
    return lax.dot_general(a, b, (((1,), (0,)), ((), ())), preferred_element_type=F32)


def mm_t(a, b):
    return lax.dot_general(a, b, (((1,), (1,)), ((), ())), preferred_element_type=F32)


def stacked(real, imag):
    return jnp.concatenate([real, imag], 0).astype(BF16)


def beside(real, imag):
    return jnp.concatenate([real, imag], 1).astype(BF16)


def cross(x):
    h, w = x.shape[0] // 2, x.shape[1] // 2
    return x[:h, :w] - x[h:, w:], x[:h, w:] + x[h:, :w]


def times(left_stacked, right_beside):
    return cross(mm(left_stacked, right_beside))


def times_t(real, imag, right_stacked):
    return cross(mm_t(stacked(real, imag), right_stacked))


def around(outer_stacked, middle_beside):
    return times_t(*times(outer_stacked, middle_beside), outer_stacked)


def peer_order():
    offsets = [
        (min(dz, 8 - dz) + min(dy, 4 - dy), dc, dz, dy)
        for dz in range(8)
        for dy in range(4)
        for dc in range(2)
        if dz or dy or dc
    ]
    return sorted(offsets, reverse=True)


def rows_of(slab, part, q):
    return pl.ds(64 * slab + 2 * part + q, 8, stride=8)


def kernel(
    d_hbm,
    coupling_hbm,
    rows_hbm,
    count_hbm,
    conv_hbm,
    g_out,
    in_2,
    d,
    coupling,
    rows_ref,
    count_ref,
    conv_ref,
    acc,
    walk,
    product,
    end,
    into,
    relay,
    far_end,
    far_walk,
    conv_pad,
    conv_mat,
    pick,
    pick_walk,
    base,
    stage,
    out_1,
    in_1,
    out_2,
    arrived,
    answer,
    load_sem,
    chain_send,
    chain_recv,
    a2a_send,
    a2a_recv,
    lines_here,
    columns_here,
    ready,
):
    me = lax.axis_index("energy")
    slab = lax.axis_index("slab")
    peers = lax.axis_size("energy")
    n_e, n_s, orb = d.shape[1], d.shape[2], d.shape[3]
    slots = n_s * 16
    last = n_s - 1

    coupling_load = pltpu.make_async_copy(coupling_hbm, coupling, load_sem.at[0])
    slab_loads = [
        pltpu.make_async_copy(d_hbm.at[:, :, i], d.at[:, :, i], load_sem.at[1 + i])
        for i in range(n_s)
    ]
    small_loads = [
        pltpu.make_async_copy(rows_hbm, rows_ref, load_sem.at[1 + n_s]),
        pltpu.make_async_copy(count_hbm, count_ref, load_sem.at[2 + n_s]),
        pltpu.make_async_copy(conv_hbm, conv_ref, load_sem.at[3 + n_s]),
    ]
    for c in [coupling_load, slab_loads[1], slab_loads[0]] + slab_loads[2:] + small_loads:
        c.start()

    barrier = pltpu.get_barrier_semaphore()

    z, y, core = lax.div(me, 8), lax.rem(lax.div(me, 2), 4), lax.rem(me, 2)

    def others():
        for _, dc, dz, dy in peer_order():
            there = lax.rem(core + dc, 2)
            yield lax.rem(z + dz, 8) * 8 + lax.rem(y + dy, 4) * 2 + there

    for receiver, sender in ((1, 0), (2, 1), (3, 1), (3, 2), (0, 1), (2, 3)):

        @pl.when(slab == receiver)
        def _():
            pl.semaphore_signal(
                barrier, inc=1, device_id={"slab": sender}, device_id_type=MESH
            )

    odd = lax.rem(slab, 2) == 1

    def greet(semaphore, j):
        pl.semaphore_signal(semaphore, inc=1, device_id={"energy": j}, device_id_type=MESH)

    column = [lax.rem(z + k, 8) * 8 + lax.rem(me, 8) for k in (4, 3, 5, 2, 6, 1, 7)]
    plane = [z * 8 + lax.rem(lax.rem(me, 8) + k, 8) for k in range(1, 8)]

    @pl.when(odd)
    def _():
        for j in column + plane:
            greet(barrier, j)


    def coupled(i):
        x = mm(d[:, :, i].reshape(2 * n_e * orb, orb), coupling[i]).astype(BF16)
        x = x.reshape(2, n_e, orb, orb)
        return [x[:, e].reshape(2 * orb, orb) for e in range(n_e)]

    every = range(n_e)

    coupling_load.wait()
    slab_loads[1].wait()
    step = [None, coupled(1)]
    slab_loads[0].wait()
    now = [beside(d[0, e, 0], d[1, e, 0]) for e in every]

    def plus(e, i, moved):
        return [d[c, e, i].astype(F32) + moved[c] for c in range(2)]

    def keep(e, i, new):
        for c in range(2):
            acc[e, i, c] = new[c]

    second = [plus(e, 1, around(step[1][e], now[e])) for e in every]
    slab_loads[2].wait()
    step.append(coupled(2))
    slab_loads[3].wait()
    step.append(coupled(3))
    both = [
        stacked(*times(step[3][e], beside(step[2][e][:orb], step[2][e][orb:]))) for e in every
    ]
    outer = [plus(e, 3, around(step[3][e], beside(d[0, e, 2], d[1, e, 2]))) for e in every]
    for e in every:
        keep(e, 1, second[e])
        moved = around(both[e], beside(*second[e]))
        new = [outer[e][c] + moved[c] for c in range(2)]
        keep(e, 3, new)
        end[e] = beside(*new)

    around_here = len(column) + len(plane)
    first = jnp.where(odd, jnp.where(slab == 3, 1, 3) + around_here, 1)
    pl.semaphore_wait(barrier, first)

    @pl.when(odd)
    def _():
        for j in column:
            greet(lines_here, j)

    def push(src, dst, send, recv, to):
        return pltpu.make_async_remote_copy(
            src, dst, send, recv, device_id={"slab": to}, device_id_type=MESH
        )

    first_hop = [
        push(end.at[e], into.at[e], chain_send.at[e], chain_recv.at[e], 1)
        for e in range(n_e)
    ]
    far_hop = [
        (
            push(end.at[e], far_end.at[e], chain_send.at[e], chain_recv.at[2 + e], 3),
            push(product.at[e], far_walk.at[e], chain_send.at[2 + e], chain_recv.at[4 + e], 3),
        )
        for e in range(n_e)
    ]
    second_hop = [
        [
            push(relay.at[e], into.at[e], chain_send.at[2 * e + j], chain_recv.at[e], 2 + j)
            for j in range(2)
        ]
        for e in range(n_e)
    ]

    @pl.when(slab == 0)
    def _():
        for c in first_hop:
            c.start()

    @pl.when(slab == 2)
    def _():
        for pair in far_hop:
            pair[0].start()

    step[0] = coupled(0)
    for e in every:
        walk[e, 0] = step[0][e]
        now[e] = beside(step[0][e][:orb], step[0][e][orb:])
    for i in range(1, n_s):
        for e in every:
            moved = times(step[i][e], now[e])
            walk[e, i] = stacked(*moved)
            now[e] = beside(*moved)
            if i == last:
                product[e] = now[e]

    @pl.when(slab == 2)
    def _():
        for pair in far_hop:
            pair[1].start()

    for e in every:
        for c in range(2):
            acc[e, 0, c] = d[c, e, 0].astype(F32)
        keep(e, 2, plus(e, 2, around(step[2][e], beside(acc[e, 1, 0], acc[e, 1, 1]))))

    for c in small_loads:
        c.wait()

    row_at = lax.broadcasted_iota(jnp.int32, (16, orb), 0)
    lane_at = lax.broadcasted_iota(jnp.int32, (16, orb), 1)
    for i in range(n_s):
        wanted = jnp.full((16, orb), -1, jnp.int32)
        for t in range(16):
            row = jnp.where(t < count_ref[i], rows_ref[i, t], -1)
            wanted = jnp.where(row_at == t, row, wanted)
        pick[i] = jnp.where(lane_at == wanted, 1.0, 0.0).astype(BF16)

    conv_pad[...] = jnp.zeros_like(conv_pad)
    conv_pad[0:2, 0 : 2 * orb - 1] = conv_ref[...].astype(F32)
    bands = []
    for c in range(2):
        wide = jnp.broadcast_to(conv_pad[c : c + 1, :], (orb, 2 * orb))
        bands.append(pltpu.roll(wide, orb + 1, 1, stride=1, stride_axis=0)[:, :orb])
    flipped = jnp.concatenate(
        [
            jnp.concatenate([bands[0], bands[1]], 1),
            jnp.concatenate([-bands[1], bands[0]], 1),
        ],
        0,
    ).astype(BF16)
    big = (2 * orb, 2 * orb)
    row_at = lax.broadcasted_iota(jnp.int32, big, 0)
    lane_at = lax.broadcasted_iota(jnp.int32, big, 1)
    order = jnp.where(
        lane_at == lax.rem(row_at, 2) * orb + lax.div(row_at, 2), 1.0, 0.0
    ).astype(BF16)
    conv_mat[...] = mm_t(order, mm(order, flipped).astype(BF16)).astype(BF16)

    for e in every:
        for i in range(n_s):
            at = slice(16 * i, 16 * i + 16)
            own = walk[e, i]
            chosen = mm(pick[i], jnp.concatenate([own[:orb], own[orb:]], 1)).astype(BF16)
            pick_walk[e, at] = chosen[:, :orb]
            pick_walk[e, slots + 16 * i : slots + 16 * i + 16] = chosen[:, orb:]
            high = beside(acc[e, i, 0], acc[e, i, 1])
            low = beside(*[acc[e, i, c] - acc[e, i, c].astype(BF16).astype(F32) for c in range(2)])
            base[e, at] = mm(pick[i], high) + mm(pick[i], low)

    def rows_around(e, middle):
        real, imag = times(pick_walk[e], middle)
        for i in range(n_s):
            at = slice(16 * i, 16 * i + 16)
            yield i, at, times_t(real[at], imag[at], walk[e, i])

    def blocks_around(e, middle):
        mid = mm(walk[e].reshape(n_s * 2 * orb, orb), middle).reshape(n_s, 2 * orb, 2 * orb)
        for i in range(n_s):
            yield i, times_t(*cross(mid[i]), walk[e, i])

    def select(e):
        for i, at, moved in rows_around(e, into[e]):
            for c in range(2):
                part = base[e, at, c * orb : (c + 1) * orb] + moved[c]
                for q in range(2):
                    stage[rows_of(i, 2 * e + c, q), :] = part[8 * q : 8 * q + 8]

    def lines_are_here():
        pl.semaphore_wait(lines_here, len(column))
        for j in plane:
            greet(columns_here, j)

    def all_here(to):
        pl.semaphore_wait(columns_here, len(plane))
        pl.semaphore_signal(ready, inc=1, device_id={"slab": to}, device_id_type=MESH)

    @pl.when(slab == 0)
    def _():
        into[...] = jnp.zeros_like(into)

    @pl.when(slab == 1)
    def _():
        for e in every:
            first_hop[e].wait_recv()
            moved = around(walk[e, last], into[e])
            relay[e] = beside(*[acc[e, last, c] + moved[c] for c in range(2)])
            for c in second_hop[e]:
                c.start()
            if e == 0:
                lines_are_here()
        all_here(0)

    @pl.when(slab == 3)
    def _():
        lines_are_here()
        for e in every:
            far_hop[e][0].wait_recv()
            for i, at, moved in rows_around(e, far_end[e]):
                base[e, at] = base[e, at] + jnp.concatenate(moved, 1)
            for i, moved in blocks_around(e, far_end[e]):
                for c in range(2):
                    acc[e, i, c] = acc[e, i, c] + moved[c]
        all_here(2)
        for e in every:
            far_hop[e][1].wait_recv()
            pick_walk[e] = stacked(*times(pick_walk[e], far_walk[e]))
            for i in range(n_s):
                walk[e, i] = stacked(*times(walk[e, i], far_walk[e]))

    for e in every:

        @pl.when(slab >= 2)
        def _():
            second_hop[e][0].wait_recv()

        select(e)

    half = peers // 2
    mine = lax.rem(me, half)

    def send(src, dst, at, to):
        pltpu.make_async_remote_copy(
            src,
            dst,
            a2a_send.at[at],
            a2a_recv.at[at],
            device_id={"energy": to},
            device_id_type=MESH,
        ).start()

    def all_but_own(ref, count, sem):
        most = ref.at[pl.ds(0, count - 1)]
        return pltpu.make_async_copy(most, most, sem)

    out_1[...] = stage[...].astype(BF16).reshape(out_1.shape)

    @pl.when(jnp.logical_not(odd))
    def _():
        pl.semaphore_wait(ready, 1)

    for j in others():
        send(out_1.at[lax.rem(j, half)], in_1.at[me], 0, j)
    in_1[me] = out_1[mine]

    for e in every:
        for i, moved in blocks_around(e, into[e]):
            for c in range(2):
                g_out[c, e, i] = acc[e, i, c] + moved[c]

    all_but_own(in_1, peers, a2a_recv.at[0]).wait()
    arrived[...] = in_1[...].reshape(arrived.shape).astype(F32)
    for q in range(2):
        at = pl.ds(q, 4 * peers, stride=2)
        answer[at, :] = mm(conv_mat[...], arrived[at, :].astype(BF16))
    out_2[...] = answer[...].astype(BF16).reshape(out_2.shape)
    for dz in (2, 7, 1, 0):
        for dy in (2, 1, 3, 0):
            for dc in (1, 0):
                if dz or dy or dc:
                    there = lax.rem(y + dy, 4) * 2 + lax.rem(core + dc, 2)
                    j = lax.rem(z + dz, 8) * 8 + there
                    send(out_2.at[j], in_2.at[mine], 1, j)
    in_2[mine] = out_2[me]

    @pl.when(slab == 0)
    def _():
        for c in first_hop:
            c.wait_send()

    @pl.when(slab == 1)
    def _():
        for pair in second_hop:
            for c in pair:
                c.wait_send()

    @pl.when(slab == 2)
    def _():
        for pair in far_hop:
            for c in pair:
                c.wait_send()

    all_but_own(in_1, peers, a2a_send.at[0]).wait()
    all_but_own(in_2, half, a2a_recv.at[1]).wait()
    all_but_own(out_2, half, a2a_send.at[1]).wait()


def finish(g, rows, g_hbm, self_hbm, stage, self_out, sem):
    copies = [
        pltpu.make_async_copy(g, g_hbm, sem.at[0]),
        pltpu.make_async_copy(self_out, self_hbm, sem.at[1]),
    ]
    copies[0].start()
    _, n_e, n_s, _, orb = self_out.shape
    stage[...] = rows[...].reshape(stage.shape).astype(F32)
    for e in range(n_e):
        for c in range(2):
            for i in range(n_s):
                parts = [stage[rows_of(i, 2 * e + c, q), :] for q in range(2)]
                self_out[c, e, i] = jnp.concatenate(parts, 0).astype(BF16)
    copies[1].start()
    for c in copies:
        c.wait()


def on_device(inv_diag, coupling, tile_rows, tile_count, conv):
    _, n_e, n_s, orb, _ = inv_diag.shape
    slots = n_s * 16
    vmem = pl.BlockSpec(memory_space=pltpu.VMEM)
    dma = pltpu.SemaphoreType.DMA
    hbm = pl.BlockSpec(memory_space=pltpu.HBM)
    g_shape = jax.ShapeDtypeStruct(inv_diag.shape, F32)
    self_shape = jax.ShapeDtypeStruct((2, n_e, n_s, 16, orb), BF16)
    peers = lax.axis_size("energy")
    rows_shape = jax.ShapeDtypeStruct((slots // 2, 8, orb), BF16)
    g, rows = pl.pallas_call(
        kernel,
        out_shape=(g_shape, rows_shape),
        in_specs=[hbm] * 5,
        out_specs=(vmem, vmem),
        scratch_shapes=[
            pltpu.VMEM(inv_diag.shape, BF16),
            pltpu.VMEM(coupling.shape, BF16),
            pltpu.SMEM(tile_rows.shape, jnp.int32),
            pltpu.SMEM(tile_count.shape, jnp.int32),
            pltpu.VMEM(conv.shape, BF16),
            pltpu.VMEM((n_e, n_s, 2, orb, orb), F32),
            pltpu.VMEM((n_e, n_s, 2 * orb, orb), BF16),
            pltpu.VMEM((n_e, orb, 2 * orb), BF16),
            pltpu.VMEM((n_e, orb, 2 * orb), BF16),
            pltpu.VMEM((n_e, orb, 2 * orb), BF16),
            pltpu.VMEM((n_e, orb, 2 * orb), BF16),
            pltpu.VMEM((n_e, orb, 2 * orb), BF16),
            pltpu.VMEM((n_e, orb, 2 * orb), BF16),
            pltpu.VMEM((8, 2 * orb), F32),
            pltpu.VMEM((2 * orb, 2 * orb), BF16),
            pltpu.VMEM((n_s, 16, orb), BF16),
            pltpu.VMEM((n_e, 2 * slots, orb), BF16),
            pltpu.VMEM((n_e, slots, 2 * orb), F32),
            pltpu.VMEM((4 * slots, orb), F32),
            pltpu.VMEM((slots // 2, 8, orb), BF16),
            pltpu.VMEM((peers, 8, orb), BF16),
            pltpu.VMEM((peers, 8, orb), BF16),
            pltpu.VMEM((8 * peers, orb), F32),
            pltpu.VMEM((8 * peers, orb), F32),
            dma((n_s + 4,)),
            dma((4,)),
            dma((6,)),
            dma((2,)),
            dma((2,)),
            pltpu.SemaphoreType.REGULAR,
            pltpu.SemaphoreType.REGULAR,
            pltpu.SemaphoreType.REGULAR,
        ],
        compiler_params=pltpu.CompilerParams(
            collective_id=0, has_side_effects=True, vmem_limit_bytes=20 * 1024 * 1024
        ),
        name="dyson",
    )(
        *[
            pltpu.with_memory_space_constraint(x, pltpu.HBM)
            for x in (inv_diag, coupling, tile_rows, tile_count, conv)
        ]
    )
    return pl.pallas_call(
        finish,
        out_shape=(g_shape, self_shape),
        in_specs=[vmem, vmem],
        out_specs=(hbm, hbm),
        scratch_shapes=[
            pltpu.VMEM((4 * slots, orb), F32),
            pltpu.VMEM(self_shape.shape, BF16),
            dma((2,)),
        ],
        compiler_params=pltpu.CompilerParams(vmem_limit_bytes=8 * 1024 * 1024),
        name="finish",
    )(g, rows)


def solution(mesh):
    placed = (
        P(None, "energy", "slab", None, None),
        P("slab", None, None),
        P("slab", None),
        P("slab"),
        P(),
    )
    return jax.shard_map(
        on_device,
        mesh=mesh,
        in_specs=placed,
        out_specs=(P(None, "energy", "slab", None, None), P(None, "energy", "slab", None, None)),
        check_vma=False,
    )
```

```python
import functools

import jax
import jax.numpy as jnp
from jax import lax
from jax.experimental import pallas as pl
from jax.experimental.pallas import tpu as pltpu
from jax.sharding import PartitionSpec as P

MESH = pl.DeviceIdType.MESH
F32 = jnp.float32
BF16 = jnp.bfloat16


def mm(a, b):
    return lax.dot_general(a, b, (((1,), (0,)), ((), ())), preferred_element_type=F32)


def mm_t(a, b):
    return lax.dot_general(a, b, (((1,), (1,)), ((), ())), preferred_element_type=F32)


def stacked(real, imag):
    return jnp.concatenate([real, imag], 0).astype(BF16)


def beside(real, imag):
    return jnp.concatenate([real, imag], 1).astype(BF16)


def cross(x):
    h, w = x.shape[0] // 2, x.shape[1] // 2
    return x[:h, :w] - x[h:, w:], x[:h, w:] + x[h:, :w]


def times(left_stacked, right_beside):
    return cross(mm(left_stacked, right_beside))


def times_t(real, imag, right_stacked):
    return cross(mm_t(stacked(real, imag), right_stacked))


def around(outer_stacked, middle_beside):
    return times_t(*times(outer_stacked, middle_beside), outer_stacked)


def peer_order():
    offsets = [
        (min(dz, 8 - dz) + min(dy, 4 - dy), dc, dz, dy)
        for dz in range(8)
        for dy in range(4)
        for dc in range(2)
        if dz or dy or dc
    ]
    return sorted(offsets, reverse=True)


def rows_of(slab, part, q):
    return pl.ds(64 * slab + 2 * part + q, 8, stride=8)


def kernel(
    d_hbm,
    coupling_hbm,
    rows_hbm,
    count_hbm,
    conv_hbm,
    g_out,
    in_2,
    d,
    coupling,
    rows_ref,
    count_ref,
    conv_ref,
    acc,
    walk,
    product,
    end,
    into,
    relay,
    far_end,
    far_walk,
    conv_pad,
    conv_mat,
    pick,
    pick_walk,
    base,
    stage,
    out_1,
    in_1,
    out_2,
    arrived,
    answer,
    load_sem,
    chain_send,
    chain_recv,
    a2a_send,
    a2a_recv,
    columns_here,
    ready,
):
    me = lax.axis_index("energy")
    slab = lax.axis_index("slab")
    peers = lax.axis_size("energy")
    n_e, n_s, orb = d.shape[1], d.shape[2], d.shape[3]
    slots = n_s * 16
    last = n_s - 1

    coupling_load = pltpu.make_async_copy(coupling_hbm, coupling, load_sem.at[0])
    slab_loads = [
        pltpu.make_async_copy(d_hbm.at[:, :, i], d.at[:, :, i], load_sem.at[1 + i])
        for i in range(n_s)
    ]
    small_loads = [
        pltpu.make_async_copy(rows_hbm, rows_ref, load_sem.at[1 + n_s]),
        pltpu.make_async_copy(count_hbm, count_ref, load_sem.at[2 + n_s]),
        pltpu.make_async_copy(conv_hbm, conv_ref, load_sem.at[3 + n_s]),
    ]
    for c in [coupling_load, slab_loads[1], slab_loads[0]] + slab_loads[2:] + small_loads:
        c.start()

    barrier = pltpu.get_barrier_semaphore()

    z, y, core = lax.div(me, 8), lax.rem(lax.div(me, 2), 4), lax.rem(me, 2)

    def others():
        for _, dc, dz, dy in peer_order():
            there = lax.rem(core + dc, 2)
            yield lax.rem(z + dz, 8) * 8 + lax.rem(y + dy, 4) * 2 + there

    for receiver, sender in ((1, 0), (2, 1), (3, 1), (3, 2), (0, 1), (2, 3)):

        @pl.when(slab == receiver)
        def _():
            pl.semaphore_signal(
                barrier, inc=1, device_id={"slab": sender}, device_id_type=MESH
            )

    odd = lax.rem(slab, 2) == 1

    def greet(semaphore, j):
        pl.semaphore_signal(semaphore, inc=1, device_id={"energy": j}, device_id_type=MESH)

    column = [lax.rem(z + k, 8) * 8 + lax.rem(me, 8) for k in (4, 3, 5, 2, 6, 1, 7)]
    plane = [z * 8 + lax.rem(lax.rem(me, 8) + k, 8) for k in range(1, 8)]

    for j in column + plane:
        pl.semaphore_signal(
            barrier,
            inc=1,
            device_id={"energy": j, "slab": 2 * lax.div(slab, 2) + 1},
            device_id_type=MESH,
        )

    def coupled(i):
        x = mm(d[:, :, i].reshape(2 * n_e * orb, orb), coupling[i]).astype(BF16)
        x = x.reshape(2, n_e, orb, orb)
        return [x[:, e].reshape(2 * orb, orb) for e in range(n_e)]

    every = range(n_e)

    coupling_load.wait()
    slab_loads[1].wait()
    step = [None, coupled(1)]
    slab_loads[0].wait()
    now = [beside(d[0, e, 0], d[1, e, 0]) for e in every]

    def plus(e, i, moved):
        return [d[c, e, i].astype(F32) + moved[c] for c in range(2)]

    def keep(e, i, new):
        for c in range(2):
            acc[e, i, c] = new[c]

    second = [plus(e, 1, around(step[1][e], now[e])) for e in every]
    slab_loads[2].wait()
    step.append(coupled(2))
    slab_loads[3].wait()
    step.append(coupled(3))
    both = [
        stacked(*times(step[3][e], beside(step[2][e][:orb], step[2][e][orb:]))) for e in every
    ]
    outer = [plus(e, 3, around(step[3][e], beside(d[0, e, 2], d[1, e, 2]))) for e in every]
    for e in every:
        keep(e, 1, second[e])
        moved = around(both[e], beside(*second[e]))
        new = [outer[e][c] + moved[c] for c in range(2)]
        keep(e, 3, new)
        end[e] = beside(*new)

    around_here = 2 * (len(column) + len(plane))
    first = jnp.where(odd, jnp.where(slab == 3, 1, 3) + around_here, 1)
    pl.semaphore_wait(barrier, first)

    @pl.when(odd)
    def _():
        for j in plane:
            greet(columns_here, j)

    def push(src, dst, send, recv, to):
        return pltpu.make_async_remote_copy(
            src, dst, send, recv, device_id={"slab": to}, device_id_type=MESH
        )

    first_hop = [
        push(end.at[e], into.at[e], chain_send.at[e], chain_recv.at[e], 1)
        for e in range(n_e)
    ]
    far_hop = [
        (
            push(end.at[e], far_end.at[e], chain_send.at[e], chain_recv.at[2 + e], 3),
            push(product.at[e], far_walk.at[e], chain_send.at[2 + e], chain_recv.at[4 + e], 3),
        )
        for e in range(n_e)
    ]
    second_hop = [
        [
            push(relay.at[e], into.at[e], chain_send.at[2 * e + j], chain_recv.at[e], 2 + j)
            for j in range(2)
        ]
        for e in range(n_e)
    ]

    @pl.when(slab == 0)
    def _():
        for c in first_hop:
            c.start()

    @pl.when(slab == 2)
    def _():
        for pair in far_hop:
            pair[0].start()

    step[0] = coupled(0)
    for e in every:
        walk[e, 0] = step[0][e]
        now[e] = beside(step[0][e][:orb], step[0][e][orb:])
    for i in range(1, n_s):
        for e in every:
            moved = times(step[i][e], now[e])
            walk[e, i] = stacked(*moved)
            now[e] = beside(*moved)
            if i == last:
                product[e] = now[e]

    @pl.when(slab == 2)
    def _():
        for pair in far_hop:
            pair[1].start()

    for e in every:
        for c in range(2):
            acc[e, 0, c] = d[c, e, 0].astype(F32)
        keep(e, 2, plus(e, 2, around(step[2][e], beside(acc[e, 1, 0], acc[e, 1, 1]))))

    for c in small_loads:
        c.wait()

    row_at = lax.broadcasted_iota(jnp.int32, (16, orb), 0)
    lane_at = lax.broadcasted_iota(jnp.int32, (16, orb), 1)
    for i in range(n_s):
        wanted = jnp.full((16, orb), -1, jnp.int32)
        for t in range(16):
            row = jnp.where(t < count_ref[i], rows_ref[i, t], -1)
            wanted = jnp.where(row_at == t, row, wanted)
        pick[i] = jnp.where(lane_at == wanted, 1.0, 0.0).astype(BF16)

    conv_pad[...] = jnp.zeros_like(conv_pad)
    conv_pad[0:2, 0 : 2 * orb - 1] = conv_ref[...].astype(F32)
    bands = []
    for c in range(2):
        wide = jnp.broadcast_to(conv_pad[c : c + 1, :], (orb, 2 * orb))
        bands.append(pltpu.roll(wide, orb + 1, 1, stride=1, stride_axis=0)[:, :orb])
    flipped = jnp.concatenate(
        [
            jnp.concatenate([bands[0], bands[1]], 1),
            jnp.concatenate([-bands[1], bands[0]], 1),
        ],
        0,
    ).astype(BF16)
    big = (2 * orb, 2 * orb)
    row_at = lax.broadcasted_iota(jnp.int32, big, 0)
    lane_at = lax.broadcasted_iota(jnp.int32, big, 1)
    order = jnp.where(
        lane_at == lax.rem(row_at, 2) * orb + lax.div(row_at, 2), 1.0, 0.0
    ).astype(BF16)
    whole_mat = mm_t(order, mm(order, flipped).astype(BF16)).astype(BF16)
    conv_mat[: 2 * orb] = whole_mat
    conv_mat[2 * orb :] = whole_mat[:orb]

    for e in every:
        for i in range(n_s):
            at = slice(16 * i, 16 * i + 16)
            own = walk[e, i]
            chosen = mm(pick[i], jnp.concatenate([own[:orb], own[orb:]], 1)).astype(BF16)
            pick_walk[e, at] = chosen[:, :orb]
            pick_walk[e, slots + 16 * i : slots + 16 * i + 16] = chosen[:, orb:]
            high = beside(acc[e, i, 0], acc[e, i, 1])
            low = beside(*[acc[e, i, c] - acc[e, i, c].astype(BF16).astype(F32) for c in range(2)])
            base[e, at] = mm(pick[i], high) + mm(pick[i], low)

    def rows_around(e, middle):
        real, imag = times(pick_walk[e], middle)
        for i in range(n_s):
            at = slice(16 * i, 16 * i + 16)
            yield i, at, times_t(real[at], imag[at], walk[e, i])

    def blocks_around(e, middle):
        mid = mm(walk[e].reshape(n_s * 2 * orb, orb), middle).reshape(n_s, 2 * orb, 2 * orb)
        for i in range(n_s):
            yield i, times_t(*cross(mid[i]), walk[e, i])

    def select(e):
        for i, at, moved in rows_around(e, into[e]):
            for c in range(2):
                part = base[e, at, c * orb : (c + 1) * orb] + moved[c]
                for q in range(2):
                    stage[rows_of(i, 2 * e + c, q), :] = part[8 * q : 8 * q + 8]

    def all_here(to):
        pl.semaphore_wait(columns_here, len(plane))
        pl.semaphore_signal(ready, inc=1, device_id={"slab": to}, device_id_type=MESH)

    @pl.when(slab == 0)
    def _():
        into[...] = jnp.zeros_like(into)

    @pl.when(slab == 1)
    def _():
        for e in every:
            first_hop[e].wait_recv()
            moved = around(walk[e, last], into[e])
            relay[e] = beside(*[acc[e, last, c] + moved[c] for c in range(2)])
            for c in second_hop[e]:
                c.start()
        all_here(0)

    @pl.when(slab == 3)
    def _():
        all_here(2)
        for e in every:
            far_hop[e][0].wait_recv()
            for i, at, moved in rows_around(e, far_end[e]):
                base[e, at] = base[e, at] + jnp.concatenate(moved, 1)
            for i, moved in blocks_around(e, far_end[e]):
                for c in range(2):
                    acc[e, i, c] = acc[e, i, c] + moved[c]
        for e in every:
            far_hop[e][1].wait_recv()
            pick_walk[e] = stacked(*times(pick_walk[e], far_walk[e]))
            for i in range(n_s):
                walk[e, i] = stacked(*times(walk[e, i], far_walk[e]))

    for e in every:

        @pl.when(slab >= 2)
        def _():
            second_hop[e][0].wait_recv()

        select(e)

    half = peers // 2
    mine = lax.rem(me, half)

    def send(src, dst, at, to):
        pltpu.make_async_remote_copy(
            src,
            dst,
            a2a_send.at[at],
            a2a_recv.at[at],
            device_id={"energy": to},
            device_id_type=MESH,
        ).start()

    def all_but_own(ref, count, sem):
        most = ref.at[pl.ds(0, count - 1)]
        return pltpu.make_async_copy(most, most, sem)

    out_1[...] = stage[...].astype(BF16).reshape(out_1.shape)

    @pl.when(jnp.logical_not(odd))
    def _():
        pl.semaphore_wait(ready, 1)

    for j in others():
        send(out_1.at[lax.rem(j, half)], in_1.at[me], 0, j)
    in_1[me] = out_1[mine]

    for e in every:
        for i, moved in blocks_around(e, into[e]):
            for c in range(2):
                g_out[c, e, i] = acc[e, i, c] + moved[c]

    all_but_own(in_1, peers, a2a_recv.at[0]).wait()
    arrived[...] = in_1[...].reshape(arrived.shape).astype(F32)
    own_rows = pl.ds(pl.multiple_of(lax.rem(z + 7, 8) * 32, 32), 2 * peers)
    for q in range(2):
        moved = mm(conv_mat[own_rows, :], arrived[pl.ds(q, 4 * peers, stride=2), :].astype(BF16))
        answer[pl.ds(q, 2 * peers, stride=2), :] = moved
    out_2[...] = answer[...].astype(BF16).reshape(out_2.shape)
    for dz in (2, 7, 1, 0):
        for dy in (2, 1, 3, 0):
            for dc in (1, 0):
                if dz or dy or dc:
                    there = lax.rem(y + dy, 4) * 2 + lax.rem(core + dc, 2)
                    j = lax.rem(z + dz, 8) * 8 + there
                    send(out_2.at[(dz + 1) % 8 * 8 + there], in_2.at[mine], 1, j)
    in_2[mine] = out_2[8 + lax.rem(me, 8)]

    @pl.when(slab == 0)
    def _():
        for c in first_hop:
            c.wait_send()

    @pl.when(slab == 1)
    def _():
        for pair in second_hop:
            for c in pair:
                c.wait_send()

    @pl.when(slab == 2)
    def _():
        for pair in far_hop:
            for c in pair:
                c.wait_send()

    all_but_own(in_1, peers, a2a_send.at[0]).wait()
    all_but_own(in_2, half, a2a_recv.at[1]).wait()
    all_but_own(out_2, half, a2a_send.at[1]).wait()


def finish(g, rows, g_hbm, self_hbm, stage, self_out, sem):
    copies = [
        pltpu.make_async_copy(g, g_hbm, sem.at[0]),
        pltpu.make_async_copy(self_out, self_hbm, sem.at[1]),
    ]
    copies[0].start()
    _, n_e, n_s, _, orb = self_out.shape
    stage[...] = rows[...].reshape(stage.shape).astype(F32)
    for e in range(n_e):
        for c in range(2):
            for i in range(n_s):
                parts = [stage[rows_of(i, 2 * e + c, q), :] for q in range(2)]
                self_out[c, e, i] = jnp.concatenate(parts, 0).astype(BF16)
    copies[1].start()
    for c in copies:
        c.wait()


def on_device(inv_diag, coupling, tile_rows, tile_count, conv):
    _, n_e, n_s, orb, _ = inv_diag.shape
    slots = n_s * 16
    vmem = pl.BlockSpec(memory_space=pltpu.VMEM)
    dma = pltpu.SemaphoreType.DMA
    hbm = pl.BlockSpec(memory_space=pltpu.HBM)
    g_shape = jax.ShapeDtypeStruct(inv_diag.shape, F32)
    self_shape = jax.ShapeDtypeStruct((2, n_e, n_s, 16, orb), BF16)
    peers = lax.axis_size("energy")
    rows_shape = jax.ShapeDtypeStruct((slots // 2, 8, orb), BF16)
    g, rows = pl.pallas_call(
        kernel,
        out_shape=(g_shape, rows_shape),
        in_specs=[hbm] * 5,
        out_specs=(vmem, vmem),
        scratch_shapes=[
            pltpu.VMEM(inv_diag.shape, BF16),
            pltpu.VMEM(coupling.shape, BF16),
            pltpu.SMEM(tile_rows.shape, jnp.int32),
            pltpu.SMEM(tile_count.shape, jnp.int32),
            pltpu.VMEM(conv.shape, BF16),
            pltpu.VMEM((n_e, n_s, 2, orb, orb), F32),
            pltpu.VMEM((n_e, n_s, 2 * orb, orb), BF16),
            pltpu.VMEM((n_e, orb, 2 * orb), BF16),
            pltpu.VMEM((n_e, orb, 2 * orb), BF16),
            pltpu.VMEM((n_e, orb, 2 * orb), BF16),
            pltpu.VMEM((n_e, orb, 2 * orb), BF16),
            pltpu.VMEM((n_e, orb, 2 * orb), BF16),
            pltpu.VMEM((n_e, orb, 2 * orb), BF16),
            pltpu.VMEM((8, 2 * orb), F32),
            pltpu.VMEM((3 * orb, 2 * orb), BF16),
            pltpu.VMEM((n_s, 16, orb), BF16),
            pltpu.VMEM((n_e, 2 * slots, orb), BF16),
            pltpu.VMEM((n_e, slots, 2 * orb), F32),
            pltpu.VMEM((4 * slots, orb), F32),
            pltpu.VMEM((slots // 2, 8, orb), BF16),
            pltpu.VMEM((peers, 8, orb), BF16),
            pltpu.VMEM((peers // 2, 8, orb), BF16),
            pltpu.VMEM((8 * peers, orb), F32),
            pltpu.VMEM((4 * peers, orb), F32),
            dma((n_s + 4,)),
            dma((4,)),
            dma((6,)),
            dma((2,)),
            dma((2,)),
            pltpu.SemaphoreType.REGULAR,
            pltpu.SemaphoreType.REGULAR,
        ],
        compiler_params=pltpu.CompilerParams(
            collective_id=0, has_side_effects=True, vmem_limit_bytes=20 * 1024 * 1024
        ),
        name="dyson",
    )(
        *[
            pltpu.with_memory_space_constraint(x, pltpu.HBM)
            for x in (inv_diag, coupling, tile_rows, tile_count, conv)
        ]
    )
    return pl.pallas_call(
        finish,
        out_shape=(g_shape, self_shape),
        in_specs=[vmem, vmem],
        out_specs=(hbm, hbm),
        scratch_shapes=[
            pltpu.VMEM((4 * slots, orb), F32),
            pltpu.VMEM(self_shape.shape, BF16),
            dma((2,)),
        ],
        compiler_params=pltpu.CompilerParams(vmem_limit_bytes=8 * 1024 * 1024),
        name="finish",
    )(g, rows)


def solution(mesh):
    placed = (
        P(None, "energy", "slab", None, None),
        P("slab", None, None),
        P("slab", None),
        P("slab"),
        P(),
    )
    return jax.shard_map(
        on_device,
        mesh=mesh,
        in_specs=placed,
        out_specs=(P(None, "energy", "slab", None, None), P(None, "energy", "slab", None, None)),
        check_vma=False,
    )
```

```python
import functools

import jax
import jax.numpy as jnp
from jax import lax
from jax.experimental import pallas as pl
from jax.experimental.pallas import tpu as pltpu
from jax.sharding import PartitionSpec as P

MESH = pl.DeviceIdType.MESH
F32 = jnp.float32
BF16 = jnp.bfloat16


def mm(a, b):
    return lax.dot_general(a, b, (((1,), (0,)), ((), ())), preferred_element_type=F32)


def mm_t(a, b):
    return lax.dot_general(a, b, (((1,), (1,)), ((), ())), preferred_element_type=F32)


def stacked(real, imag):
    return jnp.concatenate([real, imag], 0).astype(BF16)


def beside(real, imag):
    return jnp.concatenate([real, imag], 1).astype(BF16)


def cross(x):
    h, w = x.shape[0] // 2, x.shape[1] // 2
    return x[:h, :w] - x[h:, w:], x[:h, w:] + x[h:, :w]


def times(left_stacked, right_beside):
    return cross(mm(left_stacked, right_beside))


def times_t(real, imag, right_stacked):
    return cross(mm_t(stacked(real, imag), right_stacked))


def around(outer_stacked, middle_beside):
    return times_t(*times(outer_stacked, middle_beside), outer_stacked)


def peer_order():
    offsets = [
        (min(dz, 8 - dz) + min(dy, 4 - dy), dc, dz, dy)
        for dz in range(8)
        for dy in range(4)
        for dc in range(2)
        if dz or dy or dc
    ]
    return sorted(offsets, reverse=True)


def rows_of(slab, part, q):
    return pl.ds(64 * slab + 2 * part + q, 8, stride=8)


def kernel(
    d_hbm,
    coupling_hbm,
    rows_hbm,
    count_hbm,
    conv_hbm,
    g_out,
    in_2,
    d,
    coupling,
    rows_ref,
    count_ref,
    conv_ref,
    acc,
    walk,
    product,
    end,
    into,
    relay,
    far_end,
    far_walk,
    conv_pad,
    conv_mat,
    pick,
    pick_walk,
    base,
    stage,
    out_1,
    in_1,
    out_2,
    arrived,
    answer,
    load_sem,
    chain_send,
    chain_recv,
    a2a_send,
    a2a_recv,
    columns_here,
    ready,
):
    me = lax.axis_index("energy")
    slab = lax.axis_index("slab")
    peers = lax.axis_size("energy")
    n_e, n_s, orb = d.shape[1], d.shape[2], d.shape[3]
    slots = n_s * 16
    last = n_s - 1

    coupling_load = pltpu.make_async_copy(coupling_hbm, coupling, load_sem.at[0])
    slab_loads = [
        pltpu.make_async_copy(d_hbm.at[:, :, i], d.at[:, :, i], load_sem.at[1 + i])
        for i in range(n_s)
    ]
    small_loads = [
        pltpu.make_async_copy(rows_hbm, rows_ref, load_sem.at[1 + n_s]),
        pltpu.make_async_copy(count_hbm, count_ref, load_sem.at[2 + n_s]),
        pltpu.make_async_copy(conv_hbm, conv_ref, load_sem.at[3 + n_s]),
    ]
    for c in [coupling_load, slab_loads[1], slab_loads[0]] + slab_loads[2:] + small_loads:
        c.start()

    barrier = pltpu.get_barrier_semaphore()

    z, y, core = lax.div(me, 8), lax.rem(lax.div(me, 2), 4), lax.rem(me, 2)

    def others():
        for _, dc, dz, dy in peer_order():
            there = lax.rem(core + dc, 2)
            yield lax.rem(z + dz, 8) * 8 + lax.rem(y + dy, 4) * 2 + there

    for receiver, sender in ((1, 0), (2, 1), (3, 1), (3, 2), (0, 1), (2, 3)):

        @pl.when(slab == receiver)
        def _():
            pl.semaphore_signal(
                barrier, inc=1, device_id={"slab": sender}, device_id_type=MESH
            )

    odd = lax.rem(slab, 2) == 1

    def greet(semaphore, j):
        pl.semaphore_signal(semaphore, inc=1, device_id={"energy": j}, device_id_type=MESH)

    column = [lax.rem(z + k, 8) * 8 + lax.rem(me, 8) for k in (4, 3, 5, 2, 6, 1, 7)]
    plane = [z * 8 + lax.rem(lax.rem(me, 8) + k, 8) for k in range(1, 8)]

    for j in column + plane:
        pl.semaphore_signal(
            barrier,
            inc=1,
            device_id={"energy": j, "slab": 2 * lax.div(slab, 2) + 1},
            device_id_type=MESH,
        )

    def coupled(i):
        x = mm(d[:, :, i].reshape(2 * n_e * orb, orb), coupling[i]).astype(BF16)
        x = x.reshape(2, n_e, orb, orb)
        return [x[:, e].reshape(2 * orb, orb) for e in range(n_e)]

    every = range(n_e)

    coupling_load.wait()
    slab_loads[1].wait()
    step = [None, coupled(1)]
    slab_loads[0].wait()
    now = [beside(d[0, e, 0], d[1, e, 0]) for e in every]

    def plus(e, i, moved):
        return [d[c, e, i].astype(F32) + moved[c] for c in range(2)]

    def keep(e, i, new):
        for c in range(2):
            acc[e, i, c] = new[c]

    second = [plus(e, 1, around(step[1][e], now[e])) for e in every]
    slab_loads[2].wait()
    step.append(coupled(2))
    slab_loads[3].wait()
    step.append(coupled(3))
    both = [
        stacked(*times(step[3][e], beside(step[2][e][:orb], step[2][e][orb:]))) for e in every
    ]
    outer = [plus(e, 3, around(step[3][e], beside(d[0, e, 2], d[1, e, 2]))) for e in every]
    for e in every:
        keep(e, 1, second[e])
        moved = around(both[e], beside(*second[e]))
        new = [outer[e][c] + moved[c] for c in range(2)]
        keep(e, 3, new)
        end[e] = beside(*new)

    around_here = 2 * (len(column) + len(plane))
    first = jnp.where(odd, jnp.where(slab == 3, 1, 3) + around_here, 1)
    pl.semaphore_wait(barrier, first)

    @pl.when(odd)
    def _():
        for j in plane:
            greet(columns_here, j)

    def push(src, dst, send, recv, to):
        return pltpu.make_async_remote_copy(
            src, dst, send, recv, device_id={"slab": to}, device_id_type=MESH
        )

    first_hop = [
        push(end.at[e], into.at[e], chain_send.at[e], chain_recv.at[e], 1)
        for e in range(n_e)
    ]
    far_hop = [
        (
            push(end.at[e], far_end.at[e], chain_send.at[e], chain_recv.at[2 + e], 3),
            push(product.at[e], far_walk.at[e], chain_send.at[2 + e], chain_recv.at[4 + e], 3),
        )
        for e in range(n_e)
    ]
    second_hop = [
        [
            push(relay.at[e], into.at[e], chain_send.at[2 * e + j], chain_recv.at[e], 2 + j)
            for j in range(2)
        ]
        for e in range(n_e)
    ]

    @pl.when(slab == 0)
    def _():
        for c in first_hop:
            c.start()

    @pl.when(slab == 2)
    def _():
        for pair in far_hop:
            pair[0].start()

    step[0] = coupled(0)
    for e in every:
        walk[e, 0] = step[0][e]
        now[e] = beside(step[0][e][:orb], step[0][e][orb:])
    for i in range(1, n_s):
        for e in every:
            moved = times(step[i][e], now[e])
            walk[e, i] = stacked(*moved)
            now[e] = beside(*moved)
            if i == last:
                product[e] = now[e]

    @pl.when(slab == 2)
    def _():
        for pair in far_hop:
            pair[1].start()

    for e in every:
        for c in range(2):
            acc[e, 0, c] = d[c, e, 0].astype(F32)
        keep(e, 2, plus(e, 2, around(step[2][e], beside(acc[e, 1, 0], acc[e, 1, 1]))))

    for c in small_loads:
        c.wait()

    row_at = lax.broadcasted_iota(jnp.int32, (16, orb), 0)
    lane_at = lax.broadcasted_iota(jnp.int32, (16, orb), 1)
    for i in range(n_s):
        wanted = jnp.full((16, orb), -1, jnp.int32)
        for t in range(16):
            row = jnp.where(t < count_ref[i], rows_ref[i, t], -1)
            wanted = jnp.where(row_at == t, row, wanted)
        pick[i] = jnp.where(lane_at == wanted, 1.0, 0.0).astype(BF16)

    conv_pad[...] = jnp.zeros_like(conv_pad)
    conv_pad[0:2, 0 : 2 * orb - 1] = conv_ref[...].astype(F32)
    bands = []
    for c in range(2):
        wide = jnp.broadcast_to(conv_pad[c : c + 1, :], (orb, 2 * orb))
        bands.append(pltpu.roll(wide, orb + 1, 1, stride=1, stride_axis=0)[:, :orb])
    flipped = jnp.concatenate(
        [
            jnp.concatenate([bands[0], bands[1]], 1),
            jnp.concatenate([-bands[1], bands[0]], 1),
        ],
        0,
    ).astype(BF16)
    big = (2 * orb, 2 * orb)
    row_at = lax.broadcasted_iota(jnp.int32, big, 0)
    lane_at = lax.broadcasted_iota(jnp.int32, big, 1)
    order = jnp.where(
        lane_at == lax.rem(row_at, 2) * orb + lax.div(row_at, 2), 1.0, 0.0
    ).astype(BF16)
    whole_mat = mm_t(order, mm(order, flipped).astype(BF16)).astype(BF16)
    conv_mat[: 2 * orb] = whole_mat
    conv_mat[2 * orb :] = whole_mat[:orb]

    for e in every:
        for i in range(n_s):
            at = slice(16 * i, 16 * i + 16)
            own = walk[e, i]
            chosen = mm(pick[i], jnp.concatenate([own[:orb], own[orb:]], 1)).astype(BF16)
            pick_walk[e, at] = chosen[:, :orb]
            pick_walk[e, slots + 16 * i : slots + 16 * i + 16] = chosen[:, orb:]
            high = beside(acc[e, i, 0], acc[e, i, 1])
            low = beside(*[acc[e, i, c] - acc[e, i, c].astype(BF16).astype(F32) for c in range(2)])
            base[e, at] = mm(pick[i], high) + mm(pick[i], low)

    def rows_around(e, middle):
        real, imag = times(pick_walk[e], middle)
        for i in range(n_s):
            at = slice(16 * i, 16 * i + 16)
            yield i, at, times_t(real[at], imag[at], walk[e, i])

    def blocks_around(e, middle):
        mid = mm(walk[e].reshape(n_s * 2 * orb, orb), middle).reshape(n_s, 2 * orb, 2 * orb)
        for i in range(n_s):
            yield i, times_t(*cross(mid[i]), walk[e, i])

    def select(e):
        for i, at, moved in rows_around(e, into[e]):
            for c in range(2):
                part = base[e, at, c * orb : (c + 1) * orb] + moved[c]
                for q in range(2):
                    stage[rows_of(i, 2 * e + c, q), :] = part[8 * q : 8 * q + 8]

    def all_here(to):
        pl.semaphore_wait(columns_here, len(plane))
        pl.semaphore_signal(ready, inc=1, device_id={"slab": to}, device_id_type=MESH)

    @pl.when(slab == 0)
    def _():
        into[...] = jnp.zeros_like(into)

    @pl.when(slab == 1)
    def _():
        for e in every:
            first_hop[e].wait_recv()
            moved = around(walk[e, last], into[e])
            relay[e] = beside(*[acc[e, last, c] + moved[c] for c in range(2)])
            for c in second_hop[e]:
                c.start()
        all_here(0)

    @pl.when(slab == 3)
    def _():
        all_here(2)
        for e in every:
            far_hop[e][0].wait_recv()
            for i, at, moved in rows_around(e, far_end[e]):
                base[e, at] = base[e, at] + jnp.concatenate(moved, 1)
            for i, moved in blocks_around(e, far_end[e]):
                for c in range(2):
                    acc[e, i, c] = acc[e, i, c] + moved[c]
        for e in every:
            far_hop[e][1].wait_recv()
            pick_walk[e] = stacked(*times(pick_walk[e], far_walk[e]))
            for i in range(n_s):
                walk[e, i] = stacked(*times(walk[e, i], far_walk[e]))

    for e in every:

        @pl.when(slab >= 2)
        def _():
            second_hop[e][0].wait_recv()

        select(e)

    half = peers // 2
    mine = lax.rem(me, half)

    def send(src, dst, at, to):
        pltpu.make_async_remote_copy(
            src,
            dst,
            a2a_send.at[at],
            a2a_recv.at[at],
            device_id={"energy": to},
            device_id_type=MESH,
        ).start()

    def all_but_own(ref, count, sem):
        most = ref.at[pl.ds(0, count - 1)]
        return pltpu.make_async_copy(most, most, sem)

    out_1[...] = stage[...].astype(BF16).reshape(out_1.shape)

    @pl.when(jnp.logical_not(odd))
    def _():
        pl.semaphore_wait(ready, 1)

    for j in others():
        send(out_1.at[lax.rem(j, half)], in_1.at[me], 0, j)
    in_1[me] = out_1[mine]

    for e in every:
        for i, moved in blocks_around(e, into[e]):
            for c in range(2):
                g_out[c, e, i] = acc[e, i, c] + moved[c]

    all_but_own(in_1, peers, a2a_recv.at[0]).wait()
    arrived[...] = in_1[...].reshape(arrived.shape).astype(F32)
    own_rows = pl.ds(pl.multiple_of(lax.rem(z + 6, 8) * 32, 32), 2 * peers)
    for q in range(2):
        moved = mm(conv_mat[own_rows, :], arrived[pl.ds(q, 4 * peers, stride=2), :].astype(BF16))
        answer[pl.ds(q, 2 * peers, stride=2), :] = moved
    out_2[...] = answer[...].astype(BF16).reshape(out_2.shape)
    for dz in (6, 1, 7, 0):
        for dy in (2, 1, 3, 0):
            for dc in (1, 0):
                if dz or dy or dc:
                    there = lax.rem(y + dy, 4) * 2 + lax.rem(core + dc, 2)
                    j = lax.rem(z + dz, 8) * 8 + there
                    send(out_2.at[(dz + 2) % 8 * 8 + there], in_2.at[mine], 1, j)
    in_2[mine] = out_2[16 + lax.rem(me, 8)]

    @pl.when(slab == 0)
    def _():
        for c in first_hop:
            c.wait_send()

    @pl.when(slab == 1)
    def _():
        for pair in second_hop:
            for c in pair:
                c.wait_send()

    @pl.when(slab == 2)
    def _():
        for pair in far_hop:
            for c in pair:
                c.wait_send()

    all_but_own(in_1, peers, a2a_send.at[0]).wait()
    all_but_own(in_2, half, a2a_recv.at[1]).wait()
    all_but_own(out_2, half, a2a_send.at[1]).wait()


def finish(g, rows, g_hbm, self_hbm, stage, self_out, sem):
    copies = [
        pltpu.make_async_copy(g, g_hbm, sem.at[0]),
        pltpu.make_async_copy(self_out, self_hbm, sem.at[1]),
    ]
    copies[0].start()
    _, n_e, n_s, _, orb = self_out.shape
    stage[...] = rows[...].reshape(stage.shape).astype(F32)
    for e in range(n_e):
        for c in range(2):
            for i in range(n_s):
                parts = [stage[rows_of(i, 2 * e + c, q), :] for q in range(2)]
                self_out[c, e, i] = jnp.concatenate(parts, 0).astype(BF16)
    copies[1].start()
    for c in copies:
        c.wait()


def on_device(inv_diag, coupling, tile_rows, tile_count, conv):
    _, n_e, n_s, orb, _ = inv_diag.shape
    slots = n_s * 16
    vmem = pl.BlockSpec(memory_space=pltpu.VMEM)
    dma = pltpu.SemaphoreType.DMA
    hbm = pl.BlockSpec(memory_space=pltpu.HBM)
    g_shape = jax.ShapeDtypeStruct(inv_diag.shape, F32)
    self_shape = jax.ShapeDtypeStruct((2, n_e, n_s, 16, orb), BF16)
    peers = lax.axis_size("energy")
    rows_shape = jax.ShapeDtypeStruct((slots // 2, 8, orb), BF16)
    g, rows = pl.pallas_call(
        kernel,
        out_shape=(g_shape, rows_shape),
        in_specs=[hbm] * 5,
        out_specs=(vmem, vmem),
        scratch_shapes=[
            pltpu.VMEM(inv_diag.shape, BF16),
            pltpu.VMEM(coupling.shape, BF16),
            pltpu.SMEM(tile_rows.shape, jnp.int32),
            pltpu.SMEM(tile_count.shape, jnp.int32),
            pltpu.VMEM(conv.shape, BF16),
            pltpu.VMEM((n_e, n_s, 2, orb, orb), F32),
            pltpu.VMEM((n_e, n_s, 2 * orb, orb), BF16),
            pltpu.VMEM((n_e, orb, 2 * orb), BF16),
            pltpu.VMEM((n_e, orb, 2 * orb), BF16),
            pltpu.VMEM((n_e, orb, 2 * orb), BF16),
            pltpu.VMEM((n_e, orb, 2 * orb), BF16),
            pltpu.VMEM((n_e, orb, 2 * orb), BF16),
            pltpu.VMEM((n_e, orb, 2 * orb), BF16),
            pltpu.VMEM((8, 2 * orb), F32),
            pltpu.VMEM((3 * orb, 2 * orb), BF16),
            pltpu.VMEM((n_s, 16, orb), BF16),
            pltpu.VMEM((n_e, 2 * slots, orb), BF16),
            pltpu.VMEM((n_e, slots, 2 * orb), F32),
            pltpu.VMEM((4 * slots, orb), F32),
            pltpu.VMEM((slots // 2, 8, orb), BF16),
            pltpu.VMEM((peers, 8, orb), BF16),
            pltpu.VMEM((peers // 2, 8, orb), BF16),
            pltpu.VMEM((8 * peers, orb), F32),
            pltpu.VMEM((4 * peers, orb), F32),
            dma((n_s + 4,)),
            dma((4,)),
            dma((6,)),
            dma((2,)),
            dma((2,)),
            pltpu.SemaphoreType.REGULAR,
            pltpu.SemaphoreType.REGULAR,
        ],
        compiler_params=pltpu.CompilerParams(
            collective_id=0, has_side_effects=True, vmem_limit_bytes=20 * 1024 * 1024
        ),
        name="dyson",
    )(
        *[
            pltpu.with_memory_space_constraint(x, pltpu.HBM)
            for x in (inv_diag, coupling, tile_rows, tile_count, conv)
        ]
    )
    return pl.pallas_call(
        finish,
        out_shape=(g_shape, self_shape),
        in_specs=[vmem, vmem],
        out_specs=(hbm, hbm),
        scratch_shapes=[
            pltpu.VMEM((4 * slots, orb), F32),
            pltpu.VMEM(self_shape.shape, BF16),
            dma((2,)),
        ],
        compiler_params=pltpu.CompilerParams(vmem_limit_bytes=8 * 1024 * 1024),
        name="finish",
    )(g, rows)


def solution(mesh):
    placed = (
        P(None, "energy", "slab", None, None),
        P("slab", None, None),
        P("slab", None),
        P("slab"),
        P(),
    )
    return jax.shard_map(
        on_device,
        mesh=mesh,
        in_specs=placed,
        out_specs=(P(None, "energy", "slab", None, None), P(None, "energy", "slab", None, None)),
        check_vma=False,
    )
```
